32 devices in a mesh: rep: 2 (over x), blk: 16 (over z, y, core).
Axes of the slice: x: 2, y: 2, z: 4, core: 2. Of those that a mesh axis runs over, the one named last changes fastest.
Arguments:
- features: bfloat16 [4096, 256], P(('rep', 'blk')), may hold values from -6 to 6
- weight: bfloat16 [256, 256], replicated, may hold values from -0.375 to 0.375
- cotangent: bfloat16 [4096, 256], P(('rep', 'blk')), may hold values from -6 to 6
- tile_row: int32 [2, 16, 8, 4], P('rep', 'blk'), may hold values from 0 to 31, as said below
- tile_col: int32 [2, 16, 8, 4], P('rep', 'blk'), may hold values from 0 to 31, as said below
- tile_count: int32 [2, 16, 8], P('rep', 'blk'), may hold values from 1 to 4, as said below
- tile_vals: bfloat16 [2, 16, 8, 4, 128, 128], P('rep', 'blk'), may hold values from 0 to 0.015625
Outputs:
- activations: bfloat16 [4096, 256], P(('rep', 'blk'))
- weight_grad: float32 [256, 256], replicated
- feature_grad: bfloat16 [4096, 256], P(('rep', 'blk'))
The draws below stay inside these ranges and needn't reach their ends.
Inputs may be any that keep to these rules, and one draw needn't show every extreme that they name: In slot (r, p, t, k) the row block lies in row panel p: p * 2 <= tile_row < (p + 1) * 2. The live slots of one (r, p, t) hold distinct (tile_row, tile_col) pairs. In slot (r, p, t, k) the column block lies in column panel q = (p - 8 * r - t) mod 16: q * 2 <= tile_col < (q + 1) * 2. Slots with k >= tile_count[r, p, t] are unused. `tile_count`: the value 4 occurs in every draw.
All inputs are finite; a program needn't handle non-finite values.
Results may differ from the reference program's by a relative error of at most 0.018.
Values may be sent and summed in bfloat16 or wider, within the bound.
No kernel may reach another device: no remote copies, remote signals or barrier semaphores. Data moves between devices by JAX's collectives and lax.ppermute only.
A program may use at most 64 MiB of HBM per device.

```python
import math
import jax
import jax.numpy as jnp
from jax import lax

F = 256
TB = 128
SLAB = 128
REPS = 2
PANELS = 16
STEPS = 8
CB = 2
CAP = 4
NODES = 4096


def tile_layout(key):
    places = CB * CB
    scores = jax.random.randint(jax.random.fold_in(key, 11), (REPS, PANELS, STEPS, places), 0, 1 << 20)
    scores = scores * places + jnp.arange(places, dtype=jnp.int32)
    chosen = jnp.argsort(scores, axis=-1, stable=True)[..., :CAP]
    member = jnp.arange(REPS, dtype=jnp.int32)[:, None, None, None]
    group = jnp.arange(PANELS, dtype=jnp.int32)[None, :, None, None]
    visit = jnp.arange(STEPS, dtype=jnp.int32)[None, None, :, None]
    column_panel = (group - STEPS * member - visit) % PANELS
    return (group * CB + chosen // CB, column_panel * CB + chosen % CB)


def draw_tile_row(key, part):
    return tile_layout(key)[0].astype(jnp.int32)


def draw_tile_col(key, part):
    return tile_layout(key)[1].astype(jnp.int32)


def draw_tile_count(key, part):
    heavy = jax.random.randint(jax.random.fold_in(key, 23), (PANELS,), 0, 8) == 0
    picked = jax.random.randint(jax.random.fold_in(key, 29), (), 0, PANELS)
    heavy = heavy | (jnp.arange(PANELS, dtype=jnp.int32) == picked)
    light = jax.random.randint(jax.random.fold_in(key, 31), (REPS, PANELS, STEPS), 1, max(2, CAP // 2 + 1))
    light = jnp.minimum(light, CAP)
    return jnp.where(heavy[None, :, None], CAP, light).astype(jnp.int32)


def steps_of(stream_key, shape, split, low, high):
    gain, own = 1.0, jax.random.fold_in(stream_key, 6)
    for dim, blocks in split:
        steps = jnp.exp(jax.random.uniform(jax.random.fold_in(own, dim), (blocks,), jnp.float32, low / len(split), high / len(split)))
        gain = gain * jnp.repeat(steps, shape[dim] // blocks).reshape([-1 if axis == dim else 1 for axis in range(len(shape))])
    return gain


def normal_values(key, dims, scale, bound, shards=(), kind=jnp.bfloat16):
    entries = jax.random.normal(key, dims, jnp.float32) * scale
    if len(shards) > 0:
        entries = steps_of(key, dims, shards, -0.22, 0.18) * entries
    return jnp.clip(entries, min=-bound, max=bound).astype(kind)


def setup_inputs(seed: int = 0) -> dict:
    key_list = jax.random.split(jax.random.key(seed), 8)
    return {
        "features": normal_values(key_list[0], (NODES, F), 1.0, 6.0, ((0, 32),)),
        "weight": normal_values(key_list[1], (F, F), F ** -0.5, 0.375),
        "cotangent": normal_values(key_list[2], (NODES, F), 1.0, 6.0, ((0, 32),)),
        "tile_row": draw_tile_row(jax.random.fold_in(key_list[7], 71), 0),
        "tile_col": draw_tile_col(jax.random.fold_in(key_list[7], 71), 0),
        "tile_count": draw_tile_count(jax.random.fold_in(key_list[7], 71), 0),
        "tile_vals": jnp.clip(0.015625 * jax.random.uniform(key_list[6], (REPS, PANELS, STEPS, CAP, TB, TB), jnp.float32) ** steps_of(key_list[6], (REPS, PANELS, STEPS, CAP, TB, TB), ((0, 2), (1, 16)), -0.2, 0.2), 0.0, 0.015625).astype(jnp.bfloat16),
    }


def to_panels(nodes):
    width = nodes.shape[-1]
    return nodes.reshape(REPS, PANELS, SLAB, width).transpose(1, 0, 2, 3).reshape(PANELS * CB, TB, width)

def from_panels(blocks):
    width = blocks.shape[-1]
    return blocks.reshape(PANELS, REPS, SLAB, width).transpose(1, 0, 2, 3).reshape(NODES, width)

def block_product(source, tile_row, tile_col, tile_count, tile_vals, transpose):
    width = source.shape[-1]
    groups = REPS * PANELS
    live = (jnp.arange(CAP, dtype=jnp.int32)[None, None, None, :] < tile_count[..., None]).astype(source.dtype)
    row_ids = tile_row.reshape(groups, STEPS * CAP).astype(jnp.int32)
    col_ids = tile_col.reshape(groups, STEPS * CAP).astype(jnp.int32)
    masks = live.reshape(groups, STEPS * CAP)
    tiles = tile_vals.reshape(groups, STEPS * CAP, TB, TB)

    def visit(total, item):
        rows_here, cols_here, mask_here, tiles_here = item
        matrices = tiles_here.astype(source.dtype)
        if transpose:
            picked = source[rows_here]
            product = jnp.einsum('kji,kjf->kif', matrices, picked)
            total = total.at[cols_here].add(product * mask_here[:, None, None])
        else:
            picked = source[cols_here]
            product = jnp.einsum('kij,kjf->kif', matrices, picked)
            total = total.at[rows_here].add(product * mask_here[:, None, None])
        return (total, None)
    start = jnp.zeros((PANELS * CB, TB, width), source.dtype)
    total, _ = lax.scan(visit, start, (row_ids, col_ids, masks, tiles))
    return total

def reference(features, weight, cotangent, tile_row, tile_col, tile_count, tile_vals):
    source = to_panels(features.astype(jnp.float32))
    aggregated = from_panels(block_product(source, tile_row, tile_col, tile_count, tile_vals, False)).astype(jnp.bfloat16)
    preact = jnp.dot(aggregated, weight, preferred_element_type=jnp.float32)
    activations = jax.nn.silu(preact).astype(jnp.bfloat16)
    sigmoid_part = jax.nn.sigmoid(preact)
    slope_grad = (cotangent.astype(jnp.float32) * sigmoid_part * (1.0 + preact * (1.0 - sigmoid_part))).astype(jnp.bfloat16)
    weight_grad = jnp.dot(aggregated.T, slope_grad, preferred_element_type=jnp.float32) * (1.0 / math.sqrt(NODES))
    back_rows = jnp.dot(slope_grad, weight.T, preferred_element_type=jnp.float32).astype(jnp.bfloat16)
    back_source = to_panels(back_rows.astype(jnp.float32))
    feature_grad = from_panels(block_product(back_source, tile_row, tile_col, tile_count, tile_vals, True)).astype(jnp.bfloat16)
    return (activations, weight_grad, feature_grad)
```

```python
import functools
import math

import jax
import jax.numpy as jnp
from jax import lax
from jax.experimental import pallas as pl
from jax.experimental.pallas import tpu as pltpu
from jax.sharding import PartitionSpec as P

BOTH = ("rep", "blk")


def xor_pairs(count, bit):
    return [(i, i ^ bit) for i in range(count)]


def tree_sum(terms):
    terms = list(terms)
    while len(terms) > 1:
        terms = [terms[i] + terms[i + 1] for i in range(0, len(terms), 2)]
    return terms[0]


def limit_for(*arrays):
    total = sum(math.prod(a.shape) * a.dtype.itemsize for a in arrays)
    return int(2 * total + (8 << 20))


def like(shape, dtype):
    return jax.ShapeDtypeStruct(shape, dtype)


def panel_slots(groups, panels, steps):
    def device(member, panel):
        return member * panels + panel % panels

    def moves(members, shift_of, odd_only=False):
        return [
            (device(m, p), device(m, p + shift_of(m)))
            for m in members
            for p in range(panels)
            if not (odd_only and p % 2 == 0)
        ]

    first = moves(range(1, groups), lambda m: steps * m)
    last = moves(range(groups - 1), lambda m: steps * (m + 1), odd_only=True)
    slots = []
    if groups == 2:
        slots.append((first + last, lambda m: steps, lambda m: m >= 0))
    else:
        slots.append((first, lambda m: steps * m, lambda m: m >= 1))
        slots.append((last, lambda m: steps * (m + 1), lambda m: m <= groups - 2))
    for k in range(1, steps // 2):
        shift = functools.partial(lambda k, m: steps * m + 2 * k, k)
        slots.append((moves(range(groups), shift), shift, lambda m: m >= 0))
    return slots


def place_kernel(step_of, rows, cols, counts, own_tiles, pass_tiles, own_ref, pass_ref):
    slot = pl.program_id(0)
    slots = pl.num_programs(0)
    cap, size = own_tiles.shape[1], own_tiles.shape[2]
    for which, tiles, out in ((0, own_tiles, own_ref), (1, pass_tiles, pass_ref)):
        step = step_of[which * slots + slot]
        there = jnp.maximum(step, 0)
        out[...] = jnp.zeros_like(out)
        for k in range(cap):

            @pl.when((step >= 0) & (k < counts[there]))
            def _():
                row = pl.multiple_of(rows[there * cap + k] * size, size)
                col = pl.multiple_of(cols[there * cap + k] * size, size)
                out[0, pl.ds(row, size), pl.ds(col, size)] = tiles[0, k]


def place_tiles(step_of, rows, cols, counts, tiles, span):
    slots = step_of.shape[0] // 2
    steps, cap, size, _ = tiles.shape
    block = (1, cap, size, size)

    def at(which):
        return pl.BlockSpec(
            block, lambda s, so, *_: (jnp.maximum(so[which * slots + s], 0), 0, 0, 0)
        )

    out = like((slots, span, span), tiles.dtype)
    return pl.pallas_call(
        place_kernel,
        grid_spec=pltpu.PrefetchScalarGridSpec(
            num_scalar_prefetch=4,
            grid=(slots,),
            in_specs=[at(0), at(1)],
            out_specs=[pl.BlockSpec((1, span, span), lambda s, *_: (s, 0, 0))] * 2,
        ),
        out_shape=[out, out],
        cost_estimate=pl.CostEstimate(
            flops=0, bytes_accessed=4 * slots * span * span * 2, transcendentals=0
        ),
        name="place_tiles",
    )(step_of, rows.reshape(-1), cols.reshape(-1), counts, tiles, tiles)


def gather_kernel(slots, groups, own_a, sib_a, *refs):
    slabs, (own_out, sib_out) = refs[:-2], refs[-2:]
    own = sib = None
    for s in range(slots):
        panel = jnp.concatenate([slabs[s * groups + i][...] for i in range(groups)], axis=0)
        a = jnp.dot(own_a[s], panel, preferred_element_type=jnp.float32)
        b = jnp.dot(sib_a[s], panel, preferred_element_type=jnp.float32)
        own = a if own is None else own + a
        sib = b if sib is None else sib + b
    own_out[...] = own
    sib_out[...] = sib.astype(sib_out.dtype)


def forward_product(own_a, sib_a, slabs, groups):
    slots, span, _ = own_a.shape
    width = slabs[0].shape[1]
    return pl.pallas_call(
        functools.partial(gather_kernel, slots, groups),
        out_shape=[like((span, width), jnp.float32), like((span, width), jnp.bfloat16)],
        compiler_params=pltpu.CompilerParams(vmem_limit_bytes=limit_for(own_a, sib_a, *slabs)),
        cost_estimate=pl.CostEstimate(
            flops=4 * slots * span * span * width,
            bytes_accessed=4 * slots * span * span,
            transcendentals=0,
        ),
        name="forward_product",
    )(own_a, sib_a, *slabs)


def layer_kernel(groups, core, first, second, weight, *refs):
    cots, (act_out, keep_out, pass_out, back_out, grad) = refs[:groups], refs[groups:]
    size = cots[0].shape[0]
    half = keep_out.shape[0]
    grads = []
    for i in range(groups):
        here = pl.ds(i * size, size)
        there = pl.ds((i ^ (groups // 2)) * size, size)
        total = first[here, :].astype(jnp.float32) + second[there, :].astype(jnp.float32)
        aggregated = total.astype(jnp.bfloat16)
        preact = jnp.dot(aggregated, weight[...], preferred_element_type=jnp.float32)
        s = 1.0 / (1.0 + jnp.exp(-preact))
        if i == 0:
            act_out[...] = (preact * s).astype(act_out.dtype)
        slope = cots[i][...].astype(jnp.float32) * s * (1.0 + preact * (1.0 - s))
        slope = slope.astype(jnp.bfloat16)
        grads.append(
            lax.dot_general(
                aggregated, slope, (((0,), (0,)), ((), ())), preferred_element_type=jnp.float32
            )
        )
        back = lax.dot_general(
            slope, weight[...], (((1,), (1,)), ((), ())), preferred_element_type=jnp.float32
        )
        back_out[here, :] = back.astype(back_out.dtype)
    grad[...] = tree_sum(grads)
    keep = pl.multiple_of(core[0] * half, half)
    away = pl.multiple_of((1 - core[0]) * half, half)
    keep_out[...] = grad[pl.ds(keep, half), :].astype(keep_out.dtype)
    pass_out[...] = grad[pl.ds(away, half), :].astype(pass_out.dtype)


def layer(core, first, second, weight, cots, groups):
    span, width = first.shape
    size = cots[0].shape[0]
    whole = pl.BlockSpec(memory_space=pltpu.VMEM)
    return pl.pallas_call(
        functools.partial(layer_kernel, groups),
        in_specs=[pl.BlockSpec(memory_space=pltpu.SMEM)] + [whole] * (3 + groups),
        out_shape=[
            like((size, width), jnp.bfloat16),
            like((width // 2, width), jnp.bfloat16),
            like((width // 2, width), jnp.bfloat16),
            like((span, width), jnp.bfloat16),
        ],
        scratch_shapes=[pltpu.VMEM((width, width), jnp.float32)],
        compiler_params=pltpu.CompilerParams(vmem_limit_bytes=limit_for(first, second, *cots)),
        cost_estimate=pl.CostEstimate(
            flops=6 * span * width * width,
            bytes_accessed=8 * span * width,
            transcendentals=span * width,
        ),
        name="layer",
    )(core, first, second, weight, *cots)


def scatter_kernel(slots, own_a, sib_a, own_rows, sib_rows, *outs):
    for s in range(slots):
        turned = (((0,), (0,)), ((), ()))
        total = lax.dot_general(
            own_a[s], own_rows[...], turned, preferred_element_type=jnp.float32
        ) + lax.dot_general(sib_a[s], sib_rows[...], turned, preferred_element_type=jnp.float32)
        outs[s][...] = total.astype(outs[s].dtype)


def backward_product(own_a, sib_a, own_rows, sib_rows):
    slots, span, _ = own_a.shape
    width = own_rows.shape[1]
    return pl.pallas_call(
        functools.partial(scatter_kernel, slots),
        out_shape=[
            like((span, width), jnp.float32 if s == 0 else jnp.bfloat16) for s in range(slots)
        ],
        compiler_params=pltpu.CompilerParams(
            vmem_limit_bytes=limit_for(own_a, sib_a) + slots * span * width * 8
        ),
        cost_estimate=pl.CostEstimate(
            flops=4 * slots * span * span * width,
            bytes_accessed=4 * slots * span * span,
            transcendentals=0,
        ),
        name="backward_product",
    )(own_a, sib_a, own_rows, sib_rows)


def on_device(features, weight, cotangent, tile_row, tile_col, tile_count, tile_vals):
    size, width = features.shape
    groups = lax.axis_size("rep")
    panels = lax.axis_size("blk")
    steps = panels // groups
    span = groups * size
    member = lax.axis_index("rep")
    panel = lax.axis_index("blk")
    core = panel % 2
    slots = panel_slots(groups, panels, steps)

    def across(array, bit):
        return lax.ppermute(array, "rep", xor_pairs(groups, bit))

    def along(array, bit):
        return lax.ppermute(array, "blk", xor_pairs(panels, bit))

    slabs = [features] + [across(features, i) for i in range(1, groups)]
    cots = [cotangent] + [across(cotangent, i) for i in range(1, groups)]

    shifts = [(jnp.int32(0), True)] + [(shift(member), had(member)) for _, shift, had in slots]
    own_steps, pass_steps = [], []
    for shift, had in shifts:
        for offset, into in ((0, own_steps), (2 * core - 1, pass_steps)):
            step = (shift - steps * member + offset) % panels
            into.append(jnp.where((step < steps) & had, step, -1))
    step_of = jnp.stack(own_steps + pass_steps).astype(jnp.int32)
    own_a, pass_a = place_tiles(
        step_of,
        (tile_row[0, 0] % groups) ^ member,
        (tile_col[0, 0] % groups) ^ member,
        tile_count[0, 0],
        tile_vals[0, 0],
        span,
    )
    sib_a = along(pass_a, 1)

    held = list(slabs)
    for pairs, _, _ in slots:
        held += [lax.ppermute(slab, BOTH, pairs) for slab in slabs]
    own_part, sib_part = forward_product(own_a, sib_a, held, groups)
    total = (own_part + along(sib_part, 1).astype(jnp.float32)).astype(jnp.bfloat16)
    bit = 1
    while 2 * bit < groups:
        moved = across(total, bit).reshape(groups, size, width)
        moved = moved[jnp.arange(groups) ^ bit].reshape(span, width)
        total = (total.astype(jnp.float32) + moved.astype(jnp.float32)).astype(jnp.bfloat16)
        bit *= 2
    other = across(total, bit)

    activations, grad_keep, grad_pass, back_rows = layer(
        core.reshape(1).astype(jnp.int32), total, other, weight, cots, groups
    )
    parts = backward_product(own_a, sib_a, back_rows, along(back_rows, 1))

    grad = (grad_keep.astype(jnp.float32) + along(grad_pass, 1).astype(jnp.float32)).astype(
        jnp.bfloat16
    )
    bit = 2
    while bit < panels:
        grad = (grad.astype(jnp.float32) + along(grad, bit).astype(jnp.float32)).astype(
            jnp.bfloat16
        )
        bit *= 2
    mate = along(grad, 1)
    weight_grad = jnp.where(
        core == 0, jnp.concatenate([grad, mate]), jnp.concatenate([mate, grad])
    ).astype(jnp.float32) * (1.0 / math.sqrt(size * groups * panels))

    column = parts[0]
    for (pairs, _, _), part in zip(slots, parts[1:]):
        column = column + lax.ppermute(part, BOTH, [(b, a) for a, b in pairs]).astype(jnp.float32)
    column = column.reshape(groups, size, width)
    feature_grad = column[0]
    for i in range(1, groups):
        feature_grad = feature_grad + across(column[i].astype(jnp.bfloat16), i).astype(jnp.float32)
    return activations, weight_grad, feature_grad.astype(jnp.bfloat16)


def solution(mesh):
    return jax.shard_map(
        on_device,
        mesh=mesh,
        in_specs=(
            P(BOTH, None),
            P(),
            P(BOTH, None),
            P("rep", "blk", None, None),
            P("rep", "blk", None, None),
            P("rep", "blk", None),
            P("rep", "blk", None, None, None, None),
        ),
        out_specs=(P(BOTH, None), P(), P(BOTH, None)),
        check_vma=False,
    )
```

```python
import functools
import math

import jax
import jax.numpy as jnp
from jax import lax
from jax.experimental import pallas as pl
from jax.experimental.pallas import tpu as pltpu
from jax.sharding import PartitionSpec as P

BOTH = ("rep", "blk")


def xor_pairs(count, bit):
    return [(i, i ^ bit) for i in range(count)]


def tree_sum(terms):
    terms = list(terms)
    while len(terms) > 1:
        terms = [terms[i] + terms[i + 1] for i in range(0, len(terms), 2)]
    return terms[0]


def limit_for(*arrays):
    total = sum(math.prod(a.shape) * a.dtype.itemsize for a in arrays)
    return int(2 * total + (8 << 20))


def like(shape, dtype):
    return jax.ShapeDtypeStruct(shape, dtype)


def after(value, *others):
    return lax.optimization_barrier((value,) + others)[0]


def pairs_of(groups, panels, target, members=None, odd_only=False):
    return [
        (m * panels + p, m * panels + target(m, p) % panels)
        for m in (range(groups) if members is None else members)
        for p in range(panels)
        if not (odd_only and p % 2 == 0)
    ]


def back(pairs):
    return [(b, a) for a, b in pairs]


def move(array, pairs):
    return lax.ppermute(array, BOTH, pairs)


def across(array, bit):
    return lax.ppermute(array, "rep", xor_pairs(lax.axis_size("rep"), bit))


def along(array, bit):
    return lax.ppermute(array, "blk", xor_pairs(lax.axis_size("blk"), bit))


class Direct:
    def __init__(self, groups, panels):
        self.groups, steps = groups, panels // groups
        self.steps = steps
        first = pairs_of(groups, panels, lambda m, p: p + steps * m, range(1, groups))
        last = pairs_of(
            groups, panels, lambda m, p: p + steps * (m + 1), range(groups - 1), odd_only=True
        )
        self.moves = [first, last] + [
            pairs_of(groups, panels, functools.partial(lambda k, m, p: p + steps * m + 2 * k, k))
            for k in range(1, steps // 2)
        ]

    def shifts(self, member, panel):
        steps, groups = self.steps, self.groups
        return [
            (0, True),
            (steps * member, member >= 1),
            (steps * (member + 1), member <= groups - 2),
        ] + [(steps * member + 2 * k, True) for k in range(1, steps // 2)]

    def gather(self, slab, early, placed):
        slabs = [slab] + [across(slab, i) for i in range(1, self.groups)]
        return [slabs] + [[move(part, pairs) for part in slabs] for pairs in self.moves]

    def part_types(self):
        return [jnp.float32] + [jnp.bfloat16] * len(self.moves)

    def scatter(self, parts, size):
        column = parts[0]
        for pairs, part in zip(self.moves, parts[1:]):
            column = column + move(part, back(pairs)).astype(jnp.float32)
        total = column[:size]
        for i in range(1, self.groups):
            piece = column[i * size : (i + 1) * size].astype(jnp.bfloat16)
            total = total + across(piece, i).astype(jnp.float32)
        return total, column


class Halves:
    def __init__(self, groups, panels):
        self.panels = panels
        self.ahead = pairs_of(groups, panels, lambda m, p: p + 4 * (1 - 2 * m))
        self.cross = pairs_of(groups, panels, lambda m, p: (p ^ 2) + 4 * (1 - 2 * m))
        self.half = pairs_of(groups, panels, lambda m, p: p + panels // 2)

    @staticmethod
    def fits(groups, panels):
        return groups == 2 and panels == 8 * groups

    def shifts(self, member, panel):
        turn = 1 - 2 * member
        other = 1 - 2 * ((panel // 2) % 2)
        crossed = 4 * turn - 2 * other
        last = jnp.where(other == turn, 8 - 2 * other, -2 * other)
        return [(0, True), (self.panels // 2, True), (4 * turn, True), (crossed, True), (last, True)]

    def sends_own(self):
        return (lax.axis_index("blk") // 2) % 2 == lax.axis_index("rep")

    def gather(self, slab, early, placed):
        mate = across(slab, 1)
        far = after(move(slab, self.half), *early)
        both = jnp.concatenate([slab, mate])
        ahead = move(both, self.ahead)
        cross = move(both, self.cross)
        far_mate = across(far, 1)
        last = jnp.where(self.sends_own(), both, jnp.concatenate([far, far_mate]))
        last = along(last, 2)
        return [[both], [far, far_mate], [ahead], [cross], [last]]

    def part_types(self):
        return [jnp.float32, jnp.float32, jnp.bfloat16, jnp.bfloat16, jnp.bfloat16]

    def scatter(self, parts, size):
        own, far, ahead, cross, last = parts
        came = along(last, 2)
        ahead = move(ahead, back(self.ahead))
        cross = move(cross, back(self.cross))
        kept = self.sends_own()
        far = far + jnp.where(kept, 0.0, came.astype(jnp.float32))
        far_pass = far[size:].astype(jnp.bfloat16)
        far_sum = far[:size] + across(far_pass, 1).astype(jnp.float32)
        far_back = move(far_sum.astype(jnp.bfloat16), back(self.half))
        column = own + jnp.where(kept, after(came, far_pass).astype(jnp.float32), 0.0)
        column = column + ahead.astype(jnp.float32) + cross.astype(jnp.float32)
        mate = across(column[size:].astype(jnp.bfloat16), 1).astype(jnp.float32)
        return column[:size] + mate + far_back.astype(jnp.float32), came


def place_kernel(plan, groups, panels, *refs):
    member, panel = lax.axis_index("rep"), lax.axis_index("blk")
    shifts = plan.shifts(member, panel)
    offsets = (0, 1 - 2 * (panel % 2))
    for offset, (rows, cols, counts, tiles), out in zip(offsets, (refs[:4], refs[4:8]), refs[8:]):
        steps, cap, size, _ = tiles.shape
        for slot, (shift, had) in enumerate(shifts):
            step = lax.rem(shift - steps * member + offset + 4 * panels, panels)
            live = step < steps if had is True else (step < steps) & had
            there = jnp.where(live, step, 0)
            count = jnp.where(live, counts[there], 0)
            out[slot] = jnp.zeros(out.shape[1:], out.dtype)
            for k in range(cap):

                @pl.when(k < count)
                def _():
                    row = lax.rem(rows[k, there], groups) ^ member
                    col = lax.rem(cols[k, there], groups) ^ member
                    row = pl.multiple_of(row * size, size)
                    col = pl.multiple_of(col * size, size)
                    out[slot, pl.ds(row, size), pl.ds(col, size)] = tiles[there, k]


def place_tiles(plan, slots, own, sib, span):
    tiles = own[3]
    out = like((slots, span, span), tiles.dtype)
    scalars = pl.BlockSpec(memory_space=pltpu.SMEM)
    whole = pl.BlockSpec(memory_space=pltpu.VMEM)
    return pl.pallas_call(
        functools.partial(place_kernel, plan, lax.axis_size("rep"), lax.axis_size("blk")),
        in_specs=([scalars] * 3 + [whole]) * 2,
        out_specs=[whole] * 2,
        out_shape=[out, out],
        compiler_params=pltpu.CompilerParams(vmem_limit_bytes=limit_for(out, tiles)),
        cost_estimate=pl.CostEstimate(
            flops=0, bytes_accessed=4 * slots * span * span * 2, transcendentals=0
        ),
        name="place_tiles",
    )(*own, *sib)


def gather_kernel(counts, own_a, sib_a, *refs):
    slabs, (own_out, sib_out) = refs[:-2], refs[-2:]
    own = sib = None
    start = 0
    for s, count in enumerate(counts):
        panel = [slab[...] for slab in slabs[start : start + count]]
        start += count
        panel = panel[0] if count == 1 else jnp.concatenate(panel, axis=0)
        a = jnp.dot(own_a[s], panel, preferred_element_type=jnp.float32)
        b = jnp.dot(sib_a[s], panel, preferred_element_type=jnp.float32)
        own = a if own is None else own + a
        sib = b if sib is None else sib + b
    own_out[...] = own
    sib_out[...] = sib.astype(sib_out.dtype)


def forward_product(own_a, sib_a, held):
    slots, span, _ = own_a.shape
    slabs = [slab for slot in held for slab in slot]
    width = slabs[0].shape[1]
    return pl.pallas_call(
        functools.partial(gather_kernel, [len(slot) for slot in held]),
        out_shape=[like((span, width), jnp.float32), like((span, width), jnp.bfloat16)],
        compiler_params=pltpu.CompilerParams(vmem_limit_bytes=limit_for(own_a, sib_a, *slabs)),
        cost_estimate=pl.CostEstimate(
            flops=4 * slots * span * span * width,
            bytes_accessed=4 * slots * span * span,
            transcendentals=0,
        ),
        name="forward_product",
    )(own_a, sib_a, *slabs)


def layer_kernel(groups, first, second, weight, *refs):
    core = lax.axis_index("blk") % 2
    cots, (act_out, keep_out, pass_out, back_out, grad) = refs[:groups], refs[groups:]
    size = cots[0].shape[0]
    half = keep_out.shape[0]
    grads = []
    for i in range(groups):
        here = pl.ds(i * size, size)
        there = pl.ds((i ^ (groups // 2)) * size, size)
        total = first[here, :].astype(jnp.float32) + second[there, :].astype(jnp.float32)
        aggregated = total.astype(jnp.bfloat16)
        preact = jnp.dot(aggregated, weight[...], preferred_element_type=jnp.float32)
        s = 1.0 / (1.0 + jnp.exp(-preact))
        if i == 0:
            act_out[...] = (preact * s).astype(act_out.dtype)
        slope = cots[i][...].astype(jnp.float32) * s * (1.0 + preact * (1.0 - s))
        slope = slope.astype(jnp.bfloat16)
        grads.append(
            lax.dot_general(
                aggregated, slope, (((0,), (0,)), ((), ())), preferred_element_type=jnp.float32
            )
        )
        back = lax.dot_general(
            slope, weight[...], (((1,), (1,)), ((), ())), preferred_element_type=jnp.float32
        )
        back_out[here, :] = back.astype(back_out.dtype)
    grad[...] = tree_sum(grads)
    keep = pl.multiple_of(core * half, half)
    away = pl.multiple_of((1 - core) * half, half)
    keep_out[...] = grad[pl.ds(keep, half), :].astype(keep_out.dtype)
    pass_out[...] = grad[pl.ds(away, half), :].astype(pass_out.dtype)


def layer(first, second, weight, cots, groups):
    span, width = first.shape
    size = cots[0].shape[0]
    return pl.pallas_call(
        functools.partial(layer_kernel, groups),
        out_shape=[
            like((size, width), jnp.bfloat16),
            like((width // 2, width), jnp.bfloat16),
            like((width // 2, width), jnp.bfloat16),
            like((span, width), jnp.bfloat16),
        ],
        scratch_shapes=[pltpu.VMEM((width, width), jnp.float32)],
        compiler_params=pltpu.CompilerParams(vmem_limit_bytes=limit_for(first, second, *cots)),
        cost_estimate=pl.CostEstimate(
            flops=6 * span * width * width,
            bytes_accessed=8 * span * width,
            transcendentals=span * width,
        ),
        name="layer",
    )(first, second, weight, *cots)


def scatter_kernel(own_a, sib_a, own_rows, sib_rows, *outs):
    turned = (((0,), (0,)), ((), ()))
    for s, out in enumerate(outs):
        total = lax.dot_general(
            own_a[s], own_rows[...], turned, preferred_element_type=jnp.float32
        ) + lax.dot_general(sib_a[s], sib_rows[...], turned, preferred_element_type=jnp.float32)
        out[...] = total.astype(out.dtype)


def backward_product(own_a, sib_a, own_rows, sib_rows, types):
    slots, span, _ = own_a.shape
    width = own_rows.shape[1]
    return pl.pallas_call(
        scatter_kernel,
        out_shape=[like((span, width), kind) for kind in types],
        compiler_params=pltpu.CompilerParams(
            vmem_limit_bytes=limit_for(own_a, sib_a) + slots * span * width * 8
        ),
        cost_estimate=pl.CostEstimate(
            flops=4 * slots * span * span * width,
            bytes_accessed=4 * slots * span * span,
            transcendentals=0,
        ),
        name="backward_product",
    )(own_a, sib_a, own_rows, sib_rows)


def on_device(features, weight, cotangent, tile_row, tile_col, tile_count, tile_vals):
    size, width = features.shape
    groups = lax.axis_size("rep")
    panels = lax.axis_size("blk")
    span = groups * size
    core = lax.axis_index("blk") % 2
    plan = (Halves if Halves.fits(groups, panels) else Direct)(groups, panels)
    types = plan.part_types()

    tiles = (tile_row[0, 0].T, tile_col[0, 0].T, tile_count[0, 0], tile_vals[0, 0])
    sib_tiles = [along(t, 1) for t in tiles]
    own_a, sib_a = place_tiles(plan, len(types), tiles, sib_tiles, span)
    cots = [cotangent] + [across(cotangent, i) for i in range(1, groups)]
    held = plan.gather(features, sib_tiles + cots[1:], [own_a])

    own_part, sib_part = forward_product(own_a, sib_a, held)
    total = (own_part + along(sib_part, 1).astype(jnp.float32)).astype(jnp.bfloat16)
    bit = 1
    while 2 * bit < groups:
        moved = across(total, bit).reshape(groups, size, width)
        moved = moved[jnp.arange(groups) ^ bit].reshape(span, width)
        total = (total.astype(jnp.float32) + moved.astype(jnp.float32)).astype(jnp.bfloat16)
        bit *= 2
    other = across(total, bit)

    activations, grad_keep, grad_pass, back_rows = layer(total, other, weight, cots, groups)
    sib_rows = along(back_rows, 1)
    parts = backward_product(own_a, sib_a, back_rows, sib_rows, types)
    feature_grad, came = plan.scatter(parts, size)

    grad_pass = after(grad_pass, parts[0])
    grad = (grad_keep.astype(jnp.float32) + along(grad_pass, 1).astype(jnp.float32)).astype(
        jnp.bfloat16
    )
    grad = after(grad, came)
    bit = 2
    while bit < panels:
        grad = (grad.astype(jnp.float32) + along(grad, bit).astype(jnp.float32)).astype(
            jnp.bfloat16
        )
        bit *= 2
    mate = along(grad, 1)
    weight_grad = jnp.where(
        core == 0, jnp.concatenate([grad, mate]), jnp.concatenate([mate, grad])
    ).astype(jnp.float32) * (1.0 / math.sqrt(size * groups * panels))
    return activations, weight_grad, feature_grad.astype(jnp.bfloat16)


def solution(mesh):
    return jax.shard_map(
        on_device,
        mesh=mesh,
        in_specs=(
            P(BOTH, None),
            P(),
            P(BOTH, None),
            P("rep", "blk", None, None),
            P("rep", "blk", None, None),
            P("rep", "blk", None),
            P("rep", "blk", None, None, None, None),
        ),
        out_specs=(P(BOTH, None), P(), P(BOTH, None)),
        check_vma=False,
    )
```

```python
import functools
import math

import jax
import jax.numpy as jnp
from jax import lax
from jax.experimental import pallas as pl
from jax.experimental.pallas import tpu as pltpu
from jax.sharding import PartitionSpec as P

BOTH = ("rep", "blk")


def xor_pairs(count, bit):
    return [(i, i ^ bit) for i in range(count)]


def tree_sum(terms):
    terms = list(terms)
    while len(terms) > 1:
        terms = [terms[i] + terms[i + 1] for i in range(0, len(terms), 2)]
    return terms[0]


def limit_for(*arrays):
    total = sum(math.prod(a.shape) * a.dtype.itemsize for a in arrays)
    return int(2 * total + (8 << 20))


def like(shape, dtype):
    return jax.ShapeDtypeStruct(shape, dtype)


def after(value, *others):
    return lax.optimization_barrier((value,) + others)[0]


def add_rounded(a, b):
    return (a.astype(jnp.float32) + b.astype(jnp.float32)).astype(a.dtype)


def pairs_of(groups, panels, target, members=None, odd_only=False):
    return [
        (m * panels + p, m * panels + target(m, p) % panels)
        for m in (range(groups) if members is None else members)
        for p in range(panels)
        if not (odd_only and p % 2 == 0)
    ]


def back(pairs):
    return [(b, a) for a, b in pairs]


def move(array, pairs):
    return lax.ppermute(array, BOTH, pairs)


def across(array, bit):
    return lax.ppermute(array, "rep", xor_pairs(lax.axis_size("rep"), bit))


def along(array, bit):
    return lax.ppermute(array, "blk", xor_pairs(lax.axis_size("blk"), bit))


class Direct:
    def __init__(self, groups, panels):
        self.groups, steps = groups, panels // groups
        self.steps = steps
        first = pairs_of(groups, panels, lambda m, p: p + steps * m, range(1, groups))
        last = pairs_of(
            groups, panels, lambda m, p: p + steps * (m + 1), range(groups - 1), odd_only=True
        )
        self.moves = [first, last] + [
            pairs_of(groups, panels, functools.partial(lambda k, m, p: p + steps * m + 2 * k, k))
            for k in range(1, steps // 2)
        ]

        self.batches = [list(range(1 + len(self.moves)))]

    def shifts(self, member, panel):
        steps, groups = self.steps, self.groups
        return [
            (0, True),
            (steps * member, member >= 1),
            (steps * (member + 1), member <= groups - 2),
        ] + [(steps * member + 2 * k, True) for k in range(1, steps // 2)]

    def gather(self, slab, early, placed):
        slabs = [slab] + [across(slab, i) for i in range(1, self.groups)]
        return [slabs] + [[move(part, pairs) for part in slabs] for pairs in self.moves]

    def part_types(self):
        return [jnp.float32] + [jnp.bfloat16] * len(self.moves)

    def scatter(self, parts, grad, size):
        column = parts[0]
        for pairs, part in zip(self.moves, parts[1:]):
            column = column + move(part, back(pairs)).astype(jnp.float32)
        total = column[:size]
        for i in range(1, self.groups):
            piece = column[i * size : (i + 1) * size].astype(jnp.bfloat16)
            total = total + across(piece, i).astype(jnp.float32)
        bit = 2
        while bit < lax.axis_size("blk"):
            grad = add_rounded(grad, along(grad, bit))
            bit *= 2
        return total, grad


def column_kernel(own, came, ahead, cross, keep_out, pass_out):
    size = keep_out.shape[0]
    kept = (lax.axis_index("blk") // 2) % 2 == lax.axis_index("rep")
    mine = jnp.where(kept, 1.0, 0.0)
    total = own[...] + mine * came[...].astype(jnp.float32)
    total = total + (ahead[...].astype(jnp.float32) + cross[...].astype(jnp.float32))
    keep_out[...] = total[:size]
    pass_out[...] = total[size:].astype(pass_out.dtype)


def add_column(own, came, ahead, cross, size):
    span, width = own.shape
    return pl.pallas_call(
        column_kernel,
        out_shape=[like((size, width), jnp.float32), like((span - size, width), jnp.bfloat16)],
        compiler_params=pltpu.CompilerParams(vmem_limit_bytes=limit_for(own, came, ahead, cross)),
        cost_estimate=pl.CostEstimate(
            flops=3 * span * width, bytes_accessed=8 * span * width, transcendentals=0
        ),
        name="add_column",
    )(own, came, ahead, cross)


def finish_kernel(first, second, third, out):
    total = first[...] + second[...].astype(jnp.float32) + third[...].astype(jnp.float32)
    out[...] = total.astype(out.dtype)


def finish(first, second, third):
    return pl.pallas_call(
        finish_kernel,
        out_shape=like(first.shape, second.dtype),
        compiler_params=pltpu.CompilerParams(vmem_limit_bytes=limit_for(first, second, third)),
        cost_estimate=pl.CostEstimate(
            flops=2 * first.size, bytes_accessed=8 * first.size, transcendentals=0
        ),
        name="finish",
    )(first, second, third)


def stack_kernel(first, second, out):
    size = first.shape[0]
    out[:size, :] = first[...]
    out[size:, :] = second[...]


def stack(first, second):
    size, width = first.shape
    return pl.pallas_call(
        stack_kernel,
        out_shape=like((2 * size, width), first.dtype),
        compiler_params=pltpu.CompilerParams(vmem_limit_bytes=limit_for(first, second)),
        cost_estimate=pl.CostEstimate(
            flops=0, bytes_accessed=8 * size * width, transcendentals=0
        ),
        name="stack",
    )(first, second)


class Halves:
    def __init__(self, groups, panels):
        self.panels = panels
        self.ahead = pairs_of(groups, panels, lambda m, p: p + 4 * (1 - 2 * m))
        self.cross = pairs_of(groups, panels, lambda m, p: (p ^ 2) + 4 * (1 - 2 * m))
        self.corner = [(a, b ^ panels) for a, b in pairs_of(groups, panels, lambda m, p: p ^ 2)]
        self.half = pairs_of(groups, panels, lambda m, p: p + panels // 2)

        self.batches = [[0, 2, 3], [1, 4]]

    @staticmethod
    def fits(groups, panels):
        return groups == 2 and panels == 8 * groups

    def shifts(self, member, panel):
        turn = 1 - 2 * member
        other = 1 - 2 * ((panel // 2) % 2)
        crossed = 4 * turn - 2 * other
        last = jnp.where(other == turn, 8 - 2 * other, -2 * other)
        return [(0, True), (self.panels // 2, True), (4 * turn, True), (crossed, True), (last, True)]

    def sends_own(self):
        return (lax.axis_index("blk") // 2) % 2 == lax.axis_index("rep")

    def gather(self, slab, early, placed):
        mate = across(slab, 1)
        far = after(move(slab, self.half), *early)
        both = stack(slab, mate)
        ahead = move(both, self.ahead)
        cross = move(both, self.cross)
        own = self.sends_own()
        last = along(jnp.where(own, slab, far), 2)
        last_mate = move(jnp.where(own, far, slab), self.corner)
        return [[both], [far, across(far, 1)], [ahead], [cross], [last, last_mate]]

    def part_types(self):
        return [jnp.float32, jnp.float32, jnp.bfloat16, jnp.bfloat16, jnp.bfloat16]

    def scatter(self, parts, grad, size):
        own, far, ahead, cross, last = parts
        ahead = move(ahead, back(self.ahead))
        came = along(last, 2)
        grad = add_rounded(grad, after(along(grad, 2), came))
        kept = self.sends_own()
        far = far + jnp.where(kept, 0.0, came.astype(jnp.float32))
        far_pass = far[size:].astype(jnp.bfloat16)
        far_mate = across(after(far_pass, ahead), 1)
        cross = move(cross, back(self.cross))
        grad = add_rounded(grad, after(along(grad, 4), far_mate))
        far_sum = (far[:size] + far_mate.astype(jnp.float32)).astype(jnp.bfloat16)
        far_back = move(far_sum, back(self.half))
        column, column_pass = add_column(own, came, ahead, cross, size)
        mate = across(column_pass, 1)
        grad = add_rounded(grad, after(along(grad, 8), mate, far_back))
        return finish(column, mate, far_back), grad


def place_kernel(plan, groups, panels, *refs):
    member, panel = lax.axis_index("rep"), lax.axis_index("blk")
    shifts = plan.shifts(member, panel)
    offsets = (0, 1 - 2 * (panel % 2))
    for offset, (meta, tiles), out in zip(offsets, (refs[:2], refs[2:4]), refs[4:]):
        steps, cap, size, _ = tiles.shape
        for slot, (shift, had) in enumerate(shifts):
            step = lax.rem(shift - steps * member + offset + 4 * panels, panels)
            live = step < steps if had is True else (step < steps) & had
            there = jnp.where(live, step, 0)
            count = jnp.where(live, meta[2 * cap, there], 0)
            out[slot] = jnp.zeros(out.shape[1:], out.dtype)
            for k in range(cap):

                @pl.when(k < count)
                def _():
                    row = lax.rem(meta[k, there], groups) ^ member
                    col = lax.rem(meta[cap + k, there], groups) ^ member
                    row = pl.multiple_of(row * size, size)
                    col = pl.multiple_of(col * size, size)
                    out[slot, pl.ds(row, size), pl.ds(col, size)] = tiles[there, k]


def place_tiles(plan, slots, own, sib, span):
    tiles = own[1]
    out = like((slots, span, span), tiles.dtype)
    scalars = pl.BlockSpec(memory_space=pltpu.SMEM)
    whole = pl.BlockSpec(memory_space=pltpu.VMEM)
    return pl.pallas_call(
        functools.partial(place_kernel, plan, lax.axis_size("rep"), lax.axis_size("blk")),
        in_specs=[scalars, whole] * 2,
        out_specs=[whole] * 2,
        out_shape=[out, out],
        compiler_params=pltpu.CompilerParams(vmem_limit_bytes=limit_for(out, tiles)),
        cost_estimate=pl.CostEstimate(
            flops=0, bytes_accessed=4 * slots * span * span * 2, transcendentals=0
        ),
        name="place_tiles",
    )(*own, *sib)


def gather_kernel(slots, counts, began, own_a, sib_a, *refs):
    slabs, (own_out, sib_out) = refs[:-2], refs[-2:]
    own = sib = None
    if began:
        (own_in, sib_in), slabs = slabs[:2], slabs[2:]
        own, sib = own_in[...], sib_in[...]
    start = 0
    for s, count in zip(slots, counts):
        panel = [slab[...] for slab in slabs[start : start + count]]
        start += count
        panel = panel[0] if count == 1 else jnp.concatenate(panel, axis=0)
        a = jnp.dot(own_a[s], panel, preferred_element_type=jnp.float32)
        b = jnp.dot(sib_a[s], panel, preferred_element_type=jnp.float32)
        own = a if own is None else own + a
        sib = b if sib is None else sib + b
    own_out[...] = own
    sib_out[...] = sib.astype(sib_out.dtype)


def forward_product(own_a, sib_a, held, slots, sums, last):
    _, span, _ = own_a.shape
    slabs = [slab for s in slots for slab in held[s]]
    width = slabs[0].shape[1]
    return pl.pallas_call(
        functools.partial(gather_kernel, slots, [len(held[s]) for s in slots], bool(sums)),
        out_shape=[
            like((span, width), jnp.float32),
            like((span, width), jnp.bfloat16 if last else jnp.float32),
        ],
        compiler_params=pltpu.CompilerParams(
            vmem_limit_bytes=limit_for(own_a, sib_a, *slabs, *sums)
        ),
        cost_estimate=pl.CostEstimate(
            flops=4 * len(slots) * span * span * width,
            bytes_accessed=4 * len(slots) * span * span,
            transcendentals=0,
        ),
        name="forward_product",
    )(own_a, sib_a, *sums, *slabs)


def layer_kernel(groups, first, second, weight, *refs):
    core = lax.axis_index("blk") % 2
    cots, (act_out, keep_out, sent_out, grad) = refs[:groups], refs[groups:]
    size = cots[0].shape[0]
    half = keep_out.shape[0]
    grads = []
    for i in range(groups):
        here = pl.ds(i * size, size)
        there = pl.ds((i ^ (groups // 2)) * size, size)
        total = first[here, :].astype(jnp.float32) + second[there, :].astype(jnp.float32)
        aggregated = total.astype(jnp.bfloat16)
        preact = jnp.dot(aggregated, weight[...], preferred_element_type=jnp.float32)
        s = 1.0 / (1.0 + jnp.exp(-preact))
        if i == 0:
            act_out[...] = (preact * s).astype(act_out.dtype)
        slope = cots[i][...].astype(jnp.float32) * s * (1.0 + preact * (1.0 - s))
        slope = slope.astype(jnp.bfloat16)
        grads.append(
            lax.dot_general(
                aggregated, slope, (((0,), (0,)), ((), ())), preferred_element_type=jnp.float32
            )
        )
        back = lax.dot_general(
            slope, weight[...], (((1,), (1,)), ((), ())), preferred_element_type=jnp.float32
        )
        sent_out[here, :] = back.astype(sent_out.dtype)
    grad[...] = tree_sum(grads)
    keep = pl.multiple_of(core * half, half)
    away = pl.multiple_of((1 - core) * half, half)
    keep_out[...] = grad[pl.ds(keep, half), :]
    sent_out[groups * size :, :] = grad[pl.ds(away, half), :].astype(sent_out.dtype)


def layer(first, second, weight, cots, groups):
    span, width = first.shape
    size = cots[0].shape[0]
    return pl.pallas_call(
        functools.partial(layer_kernel, groups),
        out_shape=[
            like((size, width), jnp.bfloat16),
            like((width // 2, width), jnp.float32),
            like((span + width // 2, width), jnp.bfloat16),
        ],
        scratch_shapes=[pltpu.VMEM((width, width), jnp.float32)],
        compiler_params=pltpu.CompilerParams(vmem_limit_bytes=limit_for(first, second, *cots)),
        cost_estimate=pl.CostEstimate(
            flops=6 * span * width * width,
            bytes_accessed=8 * span * width,
            transcendentals=span * width,
        ),
        name="layer",
    )(first, second, weight, *cots)


def scatter_kernel(own_a, sib_a, own_sent, sib_sent, grad, *outs):
    turned = (((0,), (0,)), ((), ()))
    span = own_a.shape[1]
    *outs, grad_out = outs
    for s, out in enumerate(outs):
        total = lax.dot_general(
            own_a[s], own_sent[:span, :], turned, preferred_element_type=jnp.float32
        ) + lax.dot_general(
            sib_a[s], sib_sent[:span, :], turned, preferred_element_type=jnp.float32
        )
        out[...] = total.astype(out.dtype)
    total = grad[...] + sib_sent[span:, :].astype(jnp.float32)
    grad_out[...] = total.astype(grad_out.dtype)


def backward_product(own_a, sib_a, own_sent, sib_sent, grad, types):
    slots, span, _ = own_a.shape
    rows, width = own_sent.shape
    outs = [like((span, width), kind) for kind in types]
    outs.append(like((rows - span, width), jnp.bfloat16))
    return pl.pallas_call(
        scatter_kernel,
        out_shape=outs,
        compiler_params=pltpu.CompilerParams(
            vmem_limit_bytes=limit_for(own_a, sib_a) + slots * span * width * 8
        ),
        cost_estimate=pl.CostEstimate(
            flops=4 * slots * span * span * width,
            bytes_accessed=4 * slots * span * span,
            transcendentals=0,
        ),
        name="backward_product",
    )(own_a, sib_a, own_sent, sib_sent, grad)


def on_device(features, weight, cotangent, tile_row, tile_col, tile_count, tile_vals):
    size, width = features.shape
    groups = lax.axis_size("rep")
    panels = lax.axis_size("blk")
    span = groups * size
    core = lax.axis_index("blk") % 2
    plan = (Halves if Halves.fits(groups, panels) else Direct)(groups, panels)
    types = plan.part_types()

    tiles = (tile_row[0, 0].T, tile_col[0, 0].T, tile_count[0, 0], tile_vals[0, 0])
    meta = jnp.concatenate([tiles[0], tiles[1], tile_count[0]])
    sib_tiles = [along(meta, 1), along(tiles[3], 1)]
    own_a, sib_a = place_tiles(plan, len(types), [meta, tiles[3]], sib_tiles, span)
    cots = [cotangent] + [across(cotangent, i) for i in range(1, groups)]
    held = plan.gather(features, sib_tiles + cots[1:], [own_a])

    sums = ()
    for slots in plan.batches:
        sums = forward_product(own_a, sib_a, held, slots, sums, slots is plan.batches[-1])
    own_part, sib_part = sums
    total = (own_part + along(sib_part, 1).astype(jnp.float32)).astype(jnp.bfloat16)
    bit = 1
    while 2 * bit < groups:
        moved = across(total, bit).reshape(groups, size, width)
        moved = moved[jnp.arange(groups) ^ bit].reshape(span, width)
        total = (total.astype(jnp.float32) + moved.astype(jnp.float32)).astype(jnp.bfloat16)
        bit *= 2
    other = across(total, bit)

    activations, grad, sent = layer(total, other, weight, cots, groups)
    *parts, grad = backward_product(own_a, sib_a, sent, along(sent, 1), grad, types)
    feature_grad, grad = plan.scatter(parts, grad, size)
    mate = along(grad, 1)
    weight_grad = jnp.where(
        core == 0, jnp.concatenate([grad, mate]), jnp.concatenate([mate, grad])
    ).astype(jnp.float32) * (1.0 / math.sqrt(size * groups * panels))
    return activations, weight_grad, feature_grad.astype(jnp.bfloat16)


def solution(mesh):
    return jax.shard_map(
        on_device,
        mesh=mesh,
        in_specs=(
            P(BOTH, None),
            P(),
            P(BOTH, None),
            P("rep", "blk", None, None),
            P("rep", "blk", None, None),
            P("rep", "blk", None),
            P("rep", "blk", None, None, None, None),
        ),
        out_specs=(P(BOTH, None), P(), P(BOTH, None)),
        check_vma=False,
    )
```

```python
import functools
import math

import jax
import jax.numpy as jnp
from jax import lax
from jax.experimental import pallas as pl
from jax.experimental.pallas import tpu as pltpu
from jax.sharding import PartitionSpec as P

BOTH = ("rep", "blk")


def xor_pairs(count, bit):
    return [(i, i ^ bit) for i in range(count)]


def tree_sum(terms):
    terms = list(terms)
    while len(terms) > 1:
        terms = [terms[i] + terms[i + 1] for i in range(0, len(terms), 2)]
    return terms[0]


def limit_for(*arrays):
    total = sum(math.prod(a.shape) * a.dtype.itemsize for a in arrays)
    return int(2 * total + (8 << 20))


def like(shape, dtype):
    return jax.ShapeDtypeStruct(shape, dtype)


def after(value, *others):
    return lax.optimization_barrier((value,) + others)[0]


def add_rounded(a, b):
    return (a.astype(jnp.float32) + b.astype(jnp.float32)).astype(a.dtype)


def pairs_of(groups, panels, target, members=None, odd_only=False):
    return [
        (m * panels + p, m * panels + target(m, p) % panels)
        for m in (range(groups) if members is None else members)
        for p in range(panels)
        if not (odd_only and p % 2 == 0)
    ]


def back(pairs):
    return [(b, a) for a, b in pairs]


def move(array, pairs):
    return lax.ppermute(array, BOTH, pairs)


def across(array, bit):
    return lax.ppermute(array, "rep", xor_pairs(lax.axis_size("rep"), bit))


def along(array, bit):
    return lax.ppermute(array, "blk", xor_pairs(lax.axis_size("blk"), bit))


class Direct:
    def __init__(self, groups, panels):
        self.groups, steps = groups, panels // groups
        self.steps = steps
        first = pairs_of(groups, panels, lambda m, p: p + steps * m, range(1, groups))
        last = pairs_of(
            groups, panels, lambda m, p: p + steps * (m + 1), range(groups - 1), odd_only=True
        )
        self.moves = [first, last] + [
            pairs_of(groups, panels, functools.partial(lambda k, m, p: p + steps * m + 2 * k, k))
            for k in range(1, steps // 2)
        ]

        self.batches = [list(range(1 + len(self.moves)))]

    def shifts(self, member, panel):
        steps, groups = self.steps, self.groups
        return [
            (0, True),
            (steps * member, member >= 1),
            (steps * (member + 1), member <= groups - 2),
        ] + [(steps * member + 2 * k, True) for k in range(1, steps // 2)]

    def gather(self, slab, cots, early):
        slabs = [slab] + [across(slab, i) for i in range(1, self.groups)]
        cots = [cots] + [across(cots, i) for i in range(1, self.groups)]
        return cots, [slabs] + [[move(part, pairs) for part in slabs] for pairs in self.moves]

    def pieces(self, size, span):
        moved = [(s, 0, span, jnp.bfloat16, False) for s in range(1, 1 + len(self.moves))]
        return [(0, 0, span, jnp.float32, False)] + moved + [(0, 0, 0, jnp.bfloat16, True)]

    def scatter(self, parts, size):
        column, grad = parts[0], parts[-1]
        for pairs, part in zip(self.moves, parts[1:-1]):
            column = column + move(part, back(pairs)).astype(jnp.float32)
        total = column[:size]
        for i in range(1, self.groups):
            piece = column[i * size : (i + 1) * size].astype(jnp.bfloat16)
            total = total + across(piece, i).astype(jnp.float32)
        bit = 2
        while bit < lax.axis_size("blk"):
            grad = add_rounded(grad, along(grad, bit))
            bit *= 2
        return total, grad


def sends_own():
    return (lax.axis_index("blk") // 2) % 2 == lax.axis_index("rep")


def far_kernel(far, far_mate, came, corner, side, far_out, grad_out):
    size = far_out.shape[0]
    slant = jnp.where(sends_own(), corner[...], came[:size, :]).astype(jnp.float32)
    total = far[...] + far_mate[...].astype(jnp.float32) + slant
    far_out[...] = total.astype(far_out.dtype)
    grad = side[size:, :].astype(jnp.float32) + came[size:, :].astype(jnp.float32)
    grad_out[...] = grad.astype(grad_out.dtype)


def column_kernel(own, came, corner, ahead, cross, keep_out, pass_out):
    size = keep_out.shape[0]
    slant = jnp.where(sends_own(), came[:size, :], corner[...]).astype(jnp.float32)
    total = own[...] + (ahead[...].astype(jnp.float32) + cross[...].astype(jnp.float32))
    keep_out[...] = total[:size] + slant
    pass_out[...] = total[size:].astype(pass_out.dtype)


def local_call(kernel, name, outs, *arrays):
    moved = sum(a.size * a.dtype.itemsize for a in arrays)
    return pl.pallas_call(
        kernel,
        out_shape=outs,
        compiler_params=pltpu.CompilerParams(vmem_limit_bytes=limit_for(*arrays)),
        cost_estimate=pl.CostEstimate(flops=moved, bytes_accessed=moved, transcendentals=0),
        name=name,
    )(*arrays)


def sort_far(far, far_mate, came, corner, side):
    rows, width = came.shape
    outs = [like(far.shape, came.dtype), like((rows - far.shape[0], width), came.dtype)]
    return local_call(far_kernel, "sort_far", outs, far, far_mate, came, corner, side)


def add_column(own, came, corner, ahead, cross):
    outs = [like(corner.shape, jnp.float32), like(corner.shape, corner.dtype)]
    return local_call(column_kernel, "add_column", outs, own, came, corner, ahead, cross)


def finish_kernel(first, second, third, out):
    total = first[...] + second[...].astype(jnp.float32) + third[...].astype(jnp.float32)
    out[...] = total.astype(out.dtype)


def finish(first, second, third):
    return pl.pallas_call(
        finish_kernel,
        out_shape=like(first.shape, second.dtype),
        compiler_params=pltpu.CompilerParams(vmem_limit_bytes=limit_for(first, second, third)),
        cost_estimate=pl.CostEstimate(
            flops=2 * first.size, bytes_accessed=8 * first.size, transcendentals=0
        ),
        name="finish",
    )(first, second, third)


def stack_kernel(first, second, out):
    size = first.shape[0]
    out[:size, :] = first[...]
    out[size:, :] = second[...]


def stack(first, second):
    size, width = first.shape
    return pl.pallas_call(
        stack_kernel,
        out_shape=like((2 * size, width), first.dtype),
        compiler_params=pltpu.CompilerParams(vmem_limit_bytes=limit_for(first, second)),
        cost_estimate=pl.CostEstimate(
            flops=0, bytes_accessed=8 * size * width, transcendentals=0
        ),
        name="stack",
    )(first, second)


class Halves:
    def __init__(self, groups, panels):
        self.panels = panels
        self.ahead = pairs_of(groups, panels, lambda m, p: p + 4 * (1 - 2 * m))
        self.cross = pairs_of(groups, panels, lambda m, p: (p ^ 2) + 4 * (1 - 2 * m))
        self.corner = [(a, b ^ panels) for a, b in pairs_of(groups, panels, lambda m, p: p ^ 2)]
        self.half = pairs_of(groups, panels, lambda m, p: p + panels // 2)

        self.batches = [[0, 2, 3], [1, 4]]

    @staticmethod
    def fits(groups, panels):
        return groups == 2 and panels == 8 * groups

    def shifts(self, member, panel):
        turn = 1 - 2 * member
        other = 1 - 2 * ((panel // 2) % 2)
        crossed = 4 * turn - 2 * other
        last = jnp.where(other == turn, 8 - 2 * other, -2 * other)
        return [(0, True), (self.panels // 2, True), (4 * turn, True), (crossed, True), (last, True)]

    def sends_own(self):
        return (lax.axis_index("blk") // 2) % 2 == lax.axis_index("rep")

    def gather(self, slab, cots, early):
        mate = across(slab, 1)
        cots = [cots, across(cots, 1)]
        far = after(move(slab, self.half), cots[1], *early)
        both = stack(slab, mate)
        ahead = move(both, self.ahead)
        cross = move(both, self.cross)
        own = self.sends_own()
        last = along(jnp.where(own, slab, far), 2)
        last_mate = move(jnp.where(own, far, slab), self.corner)
        return cots, [[both], [far, across(far, 1)], [ahead], [cross], [last, last_mate]]

    def pieces(self, size, span):
        half = jnp.bfloat16
        return [
            (0, 0, span, jnp.float32, False),
            (1, 0, size, jnp.float32, False),
            (1, size, span, half, False),
            (2, 0, span, half, False),
            (3, 0, span, half, False),
            (4, 0, size, half, True),
            (4, size, span, half, False),
        ]

    def scatter(self, parts, size):
        own, far, far_pass, ahead, cross, side, corner = parts
        ahead = move(ahead, back(self.ahead))
        cross = move(cross, back(self.cross))
        came = along(side, 2)
        corner = move(corner, back(self.corner))
        far_mate = across(far_pass, 1)
        far_sum, grad = sort_far(far, far_mate, came, corner, side)
        column, column_pass = add_column(own, came, corner, ahead, cross)
        grad = add_rounded(grad, along(grad, 4))
        far_back = move(far_sum, back(self.half))
        mate = across(column_pass, 1)
        result = finish(column, mate, far_back)
        return result, add_rounded(grad, after(along(grad, 8), result))


def place_kernel(plan, groups, panels, *refs):
    member, panel = lax.axis_index("rep"), lax.axis_index("blk")
    shifts = plan.shifts(member, panel)
    offsets = (0, 1 - 2 * (panel % 2))
    for offset, (meta, tiles), out in zip(offsets, (refs[:2], refs[2:4]), refs[4:]):
        steps, cap, size, _ = tiles.shape
        for slot, (shift, had) in enumerate(shifts):
            step = lax.rem(shift - steps * member + offset + 4 * panels, panels)
            live = step < steps if had is True else (step < steps) & had
            there = jnp.where(live, step, 0)
            count = jnp.where(live, meta[2 * cap, there], 0)
            out[slot] = jnp.zeros(out.shape[1:], out.dtype)
            for k in range(cap):

                @pl.when(k < count)
                def _():
                    row = lax.rem(meta[k, there], groups) ^ member
                    col = lax.rem(meta[cap + k, there], groups) ^ member
                    row = pl.multiple_of(row * size, size)
                    col = pl.multiple_of(col * size, size)
                    out[slot, pl.ds(row, size), pl.ds(col, size)] = tiles[there, k]


def place_tiles(plan, slots, own, sib, span):
    tiles = own[1]
    out = like((slots, span, span), tiles.dtype)
    scalars = pl.BlockSpec(memory_space=pltpu.SMEM)
    whole = pl.BlockSpec(memory_space=pltpu.VMEM)
    return pl.pallas_call(
        functools.partial(place_kernel, plan, lax.axis_size("rep"), lax.axis_size("blk")),
        in_specs=[scalars, whole] * 2,
        out_specs=[whole] * 2,
        out_shape=[out, out],
        compiler_params=pltpu.CompilerParams(vmem_limit_bytes=limit_for(out, tiles)),
        cost_estimate=pl.CostEstimate(
            flops=0, bytes_accessed=4 * slots * span * span * 2, transcendentals=0
        ),
        name="place_tiles",
    )(*own, *sib)


def gather_kernel(slots, counts, began, own_a, sib_a, *refs):
    slabs, (own_out, sib_out) = refs[:-2], refs[-2:]
    own = sib = None
    if began:
        (own_in, sib_in), slabs = slabs[:2], slabs[2:]
        own, sib = own_in[...], sib_in[...]
    start = 0
    for s, count in zip(slots, counts):
        panel = [slab[...] for slab in slabs[start : start + count]]
        start += count
        panel = panel[0] if count == 1 else jnp.concatenate(panel, axis=0)
        a = jnp.dot(own_a[s], panel, preferred_element_type=jnp.float32)
        b = jnp.dot(sib_a[s], panel, preferred_element_type=jnp.float32)
        own = a if own is None else own + a
        sib = b if sib is None else sib + b
    own_out[...] = own
    sib_out[...] = sib.astype(sib_out.dtype)


def forward_product(own_a, sib_a, held, slots, sums, last):
    _, span, _ = own_a.shape
    slabs = [slab for s in slots for slab in held[s]]
    width = slabs[0].shape[1]
    return pl.pallas_call(
        functools.partial(gather_kernel, slots, [len(held[s]) for s in slots], bool(sums)),
        out_shape=[
            like((span, width), jnp.float32),
            like((span, width), jnp.bfloat16 if last else jnp.float32),
        ],
        compiler_params=pltpu.CompilerParams(
            vmem_limit_bytes=limit_for(own_a, sib_a, *slabs, *sums)
        ),
        cost_estimate=pl.CostEstimate(
            flops=4 * len(slots) * span * span * width,
            bytes_accessed=4 * len(slots) * span * span,
            transcendentals=0,
        ),
        name="forward_product",
    )(own_a, sib_a, *sums, *slabs)


def layer_kernel(groups, first, second, weight, *refs):
    core = lax.axis_index("blk") % 2
    cots, (act_out, keep_out, sent_out, grad) = refs[:groups], refs[groups:]
    size = cots[0].shape[0]
    half = keep_out.shape[0]
    grads = []
    for i in range(groups):
        here = pl.ds(i * size, size)
        there = pl.ds((i ^ (groups // 2)) * size, size)
        total = first[here, :].astype(jnp.float32) + second[there, :].astype(jnp.float32)
        aggregated = total.astype(jnp.bfloat16)
        preact = jnp.dot(aggregated, weight[...], preferred_element_type=jnp.float32)
        s = 1.0 / (1.0 + jnp.exp(-preact))
        if i == 0:
            act_out[...] = (preact * s).astype(act_out.dtype)
        slope = cots[i][...].astype(jnp.float32) * s * (1.0 + preact * (1.0 - s))
        slope = slope.astype(jnp.bfloat16)
        grads.append(
            lax.dot_general(
                aggregated, slope, (((0,), (0,)), ((), ())), preferred_element_type=jnp.float32
            )
        )
        back = lax.dot_general(
            slope, weight[...], (((1,), (1,)), ((), ())), preferred_element_type=jnp.float32
        )
        sent_out[here, :] = back.astype(sent_out.dtype)
    grad[...] = tree_sum(grads)
    keep = pl.multiple_of(core * half, half)
    away = pl.multiple_of((1 - core) * half, half)
    keep_out[...] = grad[pl.ds(keep, half), :]
    sent_out[groups * size :, :] = grad[pl.ds(away, half), :].astype(sent_out.dtype)


def layer(first, second, weight, cots, groups):
    span, width = first.shape
    size = cots[0].shape[0]
    return pl.pallas_call(
        functools.partial(layer_kernel, groups),
        out_shape=[
            like((size, width), jnp.bfloat16),
            like((width // 2, width), jnp.float32),
            like((span + width // 2, width), jnp.bfloat16),
        ],
        scratch_shapes=[pltpu.VMEM((width, width), jnp.float32)],
        compiler_params=pltpu.CompilerParams(vmem_limit_bytes=limit_for(first, second, *cots)),
        cost_estimate=pl.CostEstimate(
            flops=6 * span * width * width,
            bytes_accessed=8 * span * width,
            transcendentals=span * width,
        ),
        name="layer",
    )(first, second, weight, *cots)


def scatter_kernel(pieces, own_a, sib_a, own_sent, sib_sent, grad, *outs):
    turned = (((0,), (0,)), ((), ()))
    slots, span, _ = own_a.shape
    for s in range(slots):
        total = lax.dot_general(
            own_a[s], own_sent[:span, :], turned, preferred_element_type=jnp.float32
        ) + lax.dot_general(
            sib_a[s], sib_sent[:span, :], turned, preferred_element_type=jnp.float32
        )
        for (slot, low, high, _, _), out in zip(pieces, outs):
            if slot == s and high > low:
                out[: high - low, :] = total[low:high].astype(out.dtype)
    total = grad[...] + sib_sent[span:, :].astype(jnp.float32)
    for (_, low, high, _, follows), out in zip(pieces, outs):
        if follows:
            out[high - low :, :] = total.astype(out.dtype)


def backward_product(own_a, sib_a, own_sent, sib_sent, grad, pieces):
    slots, span, _ = own_a.shape
    half, width = grad.shape
    return pl.pallas_call(
        functools.partial(scatter_kernel, pieces),
        out_shape=[
            like((high - low + half * follows, width), kind)
            for _, low, high, kind, follows in pieces
        ],
        compiler_params=pltpu.CompilerParams(
            vmem_limit_bytes=limit_for(own_a, sib_a) + slots * span * width * 8
        ),
        cost_estimate=pl.CostEstimate(
            flops=4 * slots * span * span * width,
            bytes_accessed=4 * slots * span * span,
            transcendentals=0,
        ),
        name="backward_product",
    )(own_a, sib_a, own_sent, sib_sent, grad)


def on_device(features, weight, cotangent, tile_row, tile_col, tile_count, tile_vals):
    size, width = features.shape
    groups = lax.axis_size("rep")
    panels = lax.axis_size("blk")
    span = groups * size
    core = lax.axis_index("blk") % 2
    plan = (Halves if Halves.fits(groups, panels) else Direct)(groups, panels)
    slots = sum(len(batch) for batch in plan.batches)

    tiles = (tile_row[0, 0].T, tile_col[0, 0].T, tile_count[0, 0], tile_vals[0, 0])
    meta = jnp.concatenate([tiles[0], tiles[1], tile_count[0]])
    sib_tiles = [along(meta, 1), along(tiles[3], 1)]
    own_a, sib_a = place_tiles(plan, slots, [meta, tiles[3]], sib_tiles, span)
    cots, held = plan.gather(features, cotangent, sib_tiles)

    sums = ()
    for batch in plan.batches:
        sums = forward_product(own_a, sib_a, held, batch, sums, batch is plan.batches[-1])
    own_part, sib_part = sums
    total = (own_part + along(sib_part, 1).astype(jnp.float32)).astype(jnp.bfloat16)
    bit = 1
    while 2 * bit < groups:
        moved = across(total, bit).reshape(groups, size, width)
        moved = moved[jnp.arange(groups) ^ bit].reshape(span, width)
        total = (total.astype(jnp.float32) + moved.astype(jnp.float32)).astype(jnp.bfloat16)
        bit *= 2
    other = across(total, bit)

    activations, grad, sent = layer(total, other, weight, cots, groups)
    pieces = plan.pieces(size, span)
    parts = backward_product(own_a, sib_a, sent, along(sent, 1), grad, pieces)
    feature_grad, grad = plan.scatter(parts, size)
    mate = along(grad, 1)
    weight_grad = jnp.where(
        core == 0, jnp.concatenate([grad, mate]), jnp.concatenate([mate, grad])
    ).astype(jnp.float32) * (1.0 / math.sqrt(size * groups * panels))
    return activations, weight_grad, feature_grad.astype(jnp.bfloat16)


def solution(mesh):
    return jax.shard_map(
        on_device,
        mesh=mesh,
        in_specs=(
            P(BOTH, None),
            P(),
            P(BOTH, None),
            P("rep", "blk", None, None),
            P("rep", "blk", None, None),
            P("rep", "blk", None),
            P("rep", "blk", None, None, None, None),
        ),
        out_specs=(P(BOTH, None), P(), P(BOTH, None)),
        check_vma=False,
    )
```

```python
import functools
import math

import jax
import jax.numpy as jnp
from jax import lax
from jax.experimental import pallas as pl
from jax.experimental.pallas import tpu as pltpu
from jax.sharding import PartitionSpec as P

BOTH = ("rep", "blk")


def xor_pairs(count, bit):
    return [(i, i ^ bit) for i in range(count)]


def tree_sum(terms):
    terms = list(terms)
    while len(terms) > 1:
        terms = [terms[i] + terms[i + 1] for i in range(0, len(terms), 2)]
    return terms[0]


def limit_for(*arrays):
    total = sum(math.prod(a.shape) * a.dtype.itemsize for a in arrays)
    return int(2 * total + (8 << 20))


def like(shape, dtype):
    return jax.ShapeDtypeStruct(shape, dtype)


def after(value, *others):
    return lax.optimization_barrier((value,) + others)[0]


def add_rounded(a, b):
    return (a.astype(jnp.float32) + b.astype(jnp.float32)).astype(a.dtype)


def pairs_of(groups, panels, target, members=None, odd_only=False):
    return [
        (m * panels + p, m * panels + target(m, p) % panels)
        for m in (range(groups) if members is None else members)
        for p in range(panels)
        if not (odd_only and p % 2 == 0)
    ]


def back(pairs):
    return [(b, a) for a, b in pairs]


def move(array, pairs):
    return lax.ppermute(array, BOTH, pairs)


def across(array, bit):
    return lax.ppermute(array, "rep", xor_pairs(lax.axis_size("rep"), bit))


def along(array, bit):
    return lax.ppermute(array, "blk", xor_pairs(lax.axis_size("blk"), bit))


class Direct:
    def __init__(self, groups, panels):
        self.groups, steps = groups, panels // groups
        self.steps = steps
        first = pairs_of(groups, panels, lambda m, p: p + steps * m, range(1, groups))
        last = pairs_of(
            groups, panels, lambda m, p: p + steps * (m + 1), range(groups - 1), odd_only=True
        )
        self.moves = [first, last] + [
            pairs_of(groups, panels, functools.partial(lambda k, m, p: p + steps * m + 2 * k, k))
            for k in range(1, steps // 2)
        ]

        self.batches = [list(range(1 + len(self.moves)))]

    def shifts(self, member, panel):
        steps, groups = self.steps, self.groups
        return [
            (0, True),
            (steps * member, member >= 1),
            (steps * (member + 1), member <= groups - 2),
        ] + [(steps * member + 2 * k, True) for k in range(1, steps // 2)]

    def gather(self, slab, cots, early):
        slabs = [slab] + [across(slab, i) for i in range(1, self.groups)]
        cots = [cots] + [across(cots, i) for i in range(1, self.groups)]
        return cots, [slabs] + [[move(part, pairs) for part in slabs] for pairs in self.moves]

    def pieces(self, size, span):
        moved = [(s, 0, span, jnp.bfloat16, False) for s in range(1, 1 + len(self.moves))]
        return [(0, 0, span, jnp.float32, False)] + moved + [(0, 0, 0, jnp.bfloat16, True)]

    def scatter(self, parts, size):
        column, grad = parts[0], parts[-1]
        for pairs, part in zip(self.moves, parts[1:-1]):
            column = column + move(part, back(pairs)).astype(jnp.float32)
        total = column[:size]
        for i in range(1, self.groups):
            piece = column[i * size : (i + 1) * size].astype(jnp.bfloat16)
            total = total + across(piece, i).astype(jnp.float32)
        bit = 2
        while bit < lax.axis_size("blk"):
            grad = add_rounded(grad, along(grad, bit))
            bit *= 2
        return total, grad


def sends_own():
    return (lax.axis_index("blk") // 2) % 2 == lax.axis_index("rep")


def far_kernel(far, far_mate, came, corner, out):
    size = out.shape[0]
    late = jnp.where(sends_own(), corner[...], came[:size, :]).astype(jnp.float32)
    out[...] = (far[...] + far_mate[...].astype(jnp.float32) + late).astype(out.dtype)


def column_kernel(own, came, corner, ahead, cross, keep_out, pass_out):
    size = keep_out.shape[0]
    slant = jnp.where(sends_own(), came[:size, :], corner[...]).astype(jnp.float32)
    total = own[...] + (ahead[...].astype(jnp.float32) + cross[...].astype(jnp.float32))
    keep_out[...] = total[:size] + slant
    pass_out[...] = total[size:].astype(pass_out.dtype)


def local_call(kernel, name, outs, *arrays):
    moved = sum(a.size * a.dtype.itemsize for a in arrays)
    return pl.pallas_call(
        kernel,
        out_shape=outs,
        compiler_params=pltpu.CompilerParams(vmem_limit_bytes=limit_for(*arrays)),
        cost_estimate=pl.CostEstimate(flops=moved, bytes_accessed=moved, transcendentals=0),
        name=name,
    )(*arrays)


def tails_kernel(first, second, out):
    size = first.shape[0] - out.shape[0]
    total = first[size:, :].astype(jnp.float32) + second[size:, :].astype(jnp.float32)
    out[...] = total.astype(out.dtype)


def add_tails(first, second, size):
    rows, width = first.shape
    return local_call(
        tails_kernel, "add_tails", like((rows - size, width), first.dtype), first, second
    )


def sort_far(far, far_mate, came, corner):
    out = like(far.shape, came.dtype)
    return local_call(far_kernel, "sort_far", out, far, far_mate, came, corner)


def add_column(own, came, corner, ahead, cross):
    outs = [like(corner.shape, jnp.float32), like(corner.shape, corner.dtype)]
    return local_call(column_kernel, "add_column", outs, own, came, corner, ahead, cross)


def finish_kernel(first, second, third, out):
    total = first[...] + second[...].astype(jnp.float32) + third[...].astype(jnp.float32)
    out[...] = total.astype(out.dtype)


def finish(first, second, third):
    return pl.pallas_call(
        finish_kernel,
        out_shape=like(first.shape, second.dtype),
        compiler_params=pltpu.CompilerParams(vmem_limit_bytes=limit_for(first, second, third)),
        cost_estimate=pl.CostEstimate(
            flops=2 * first.size, bytes_accessed=8 * first.size, transcendentals=0
        ),
        name="finish",
    )(first, second, third)


def stack_kernel(first, second, out):
    size = first.shape[0]
    out[:size, :] = first[...]
    out[size:, :] = second[...]


def stack(first, second):
    size, width = first.shape
    return pl.pallas_call(
        stack_kernel,
        out_shape=like((2 * size, width), first.dtype),
        compiler_params=pltpu.CompilerParams(vmem_limit_bytes=limit_for(first, second)),
        cost_estimate=pl.CostEstimate(
            flops=0, bytes_accessed=8 * size * width, transcendentals=0
        ),
        name="stack",
    )(first, second)


class Halves:
    def __init__(self, groups, panels):
        self.panels = panels
        self.ahead = pairs_of(groups, panels, lambda m, p: p + 4 * (1 - 2 * m))
        self.cross = pairs_of(groups, panels, lambda m, p: (p ^ 2) + 4 * (1 - 2 * m))
        self.corner = [(a, b ^ panels) for a, b in pairs_of(groups, panels, lambda m, p: p ^ 2)]
        self.half = pairs_of(groups, panels, lambda m, p: p + panels // 2)

        self.batches = [[0, 2, 3], [1, 4]]

    @staticmethod
    def fits(groups, panels):
        return groups == 2 and panels == 8 * groups

    def shifts(self, member, panel):
        turn = 1 - 2 * member
        other = 1 - 2 * ((panel // 2) % 2)
        crossed = 4 * turn - 2 * other
        last = jnp.where(other == turn, 8 - 2 * other, -2 * other)
        return [(0, True), (self.panels // 2, True), (4 * turn, True), (crossed, True), (last, True)]

    def sends_own(self):
        return (lax.axis_index("blk") // 2) % 2 == lax.axis_index("rep")

    def gather(self, slab, cots, early):
        mate = across(slab, 1)
        cots = [cots, across(cots, 1)]
        far = after(move(slab, self.half), cots[1], *early)
        both = stack(slab, mate)
        ahead = move(both, self.ahead)
        cross = move(both, self.cross)
        own = self.sends_own()
        last = along(jnp.where(own, slab, far), 2)
        last_mate = move(jnp.where(own, far, slab), self.corner)
        return cots, [[both], [far, across(far, 1)], [ahead], [cross], [last, last_mate]]

    def pieces(self, size, span):
        half = jnp.bfloat16
        return [
            (0, 0, span, jnp.float32, False),
            (1, 0, size, jnp.float32, False),
            (1, size, span, half, False),
            (2, 0, span, half, False),
            (3, 0, span, half, False),
            (4, 0, size, half, True),
            (4, size, span, half, False),
        ]

    def scatter(self, parts, size):
        own, far, far_pass, ahead, cross, side, corner = parts
        ahead = move(ahead, back(self.ahead))
        cross = move(cross, back(self.cross))
        came = along(side, 2)
        corner = move(corner, back(self.corner))
        far_mate = across(far_pass, 1)
        grad = add_tails(side, came, size)
        far_sum = sort_far(far, far_mate, came, corner)
        column, column_pass = add_column(own, came, corner, ahead, cross)
        grad = add_rounded(grad, along(grad, 4))
        far_back = move(far_sum, back(self.half))
        mate = across(column_pass, 1)
        result = finish(column, mate, far_back)
        return result, add_rounded(grad, after(along(grad, 8), result))


def place_kernel(plan, groups, panels, *refs):
    member, panel = lax.axis_index("rep"), lax.axis_index("blk")
    shifts = plan.shifts(member, panel)
    offsets = (0, 1 - 2 * (panel % 2))
    for offset, (meta, tiles), out in zip(offsets, (refs[:2], refs[2:4]), refs[4:]):
        steps, cap, size, _ = tiles.shape
        for slot, (shift, had) in enumerate(shifts):
            step = lax.rem(shift - steps * member + offset + 4 * panels, panels)
            live = step < steps if had is True else (step < steps) & had
            there = jnp.where(live, step, 0)
            count = jnp.where(live, meta[2 * cap, there], 0)
            out[slot] = jnp.zeros(out.shape[1:], out.dtype)
            for k in range(cap):

                @pl.when(k < count)
                def _():
                    row = lax.rem(meta[k, there], groups) ^ member
                    col = lax.rem(meta[cap + k, there], groups) ^ member
                    row = pl.multiple_of(row * size, size)
                    col = pl.multiple_of(col * size, size)
                    out[slot, pl.ds(row, size), pl.ds(col, size)] = tiles[there, k]


def place_tiles(plan, slots, own, sib, span):
    tiles = own[1]
    out = like((slots, span, span), tiles.dtype)
    scalars = pl.BlockSpec(memory_space=pltpu.SMEM)
    whole = pl.BlockSpec(memory_space=pltpu.VMEM)
    return pl.pallas_call(
        functools.partial(place_kernel, plan, lax.axis_size("rep"), lax.axis_size("blk")),
        in_specs=[scalars, whole] * 2,
        out_specs=[whole] * 2,
        out_shape=[out, out],
        compiler_params=pltpu.CompilerParams(vmem_limit_bytes=limit_for(out, tiles)),
        cost_estimate=pl.CostEstimate(
            flops=0, bytes_accessed=4 * slots * span * span * 2, transcendentals=0
        ),
        name="place_tiles",
    )(*own, *sib)


def gather_kernel(slots, counts, began, own_a, sib_a, *refs):
    slabs, (own_out, sib_out) = refs[:-2], refs[-2:]
    own = sib = None
    if began:
        (own_in, sib_in), slabs = slabs[:2], slabs[2:]
        own, sib = own_in[...], sib_in[...]
    start = 0
    for s, count in zip(slots, counts):
        panel = [slab[...] for slab in slabs[start : start + count]]
        start += count
        panel = panel[0] if count == 1 else jnp.concatenate(panel, axis=0)
        a = jnp.dot(own_a[s], panel, preferred_element_type=jnp.float32)
        b = jnp.dot(sib_a[s], panel, preferred_element_type=jnp.float32)
        own = a if own is None else own + a
        sib = b if sib is None else sib + b
    own_out[...] = own
    sib_out[...] = sib.astype(sib_out.dtype)


def forward_product(own_a, sib_a, held, slots, sums, last):
    _, span, _ = own_a.shape
    slabs = [slab for s in slots for slab in held[s]]
    width = slabs[0].shape[1]
    return pl.pallas_call(
        functools.partial(gather_kernel, slots, [len(held[s]) for s in slots], bool(sums)),
        out_shape=[
            like((span, width), jnp.float32),
            like((span, width), jnp.bfloat16 if last else jnp.float32),
        ],
        compiler_params=pltpu.CompilerParams(
            vmem_limit_bytes=limit_for(own_a, sib_a, *slabs, *sums)
        ),
        cost_estimate=pl.CostEstimate(
            flops=4 * len(slots) * span * span * width,
            bytes_accessed=4 * len(slots) * span * span,
            transcendentals=0,
        ),
        name="forward_product",
    )(own_a, sib_a, *sums, *slabs)


def layer_kernel(groups, first, second, weight, *refs):
    core = lax.axis_index("blk") % 2
    cots, (act_out, keep_out, sent_out, grad) = refs[:groups], refs[groups:]
    size = cots[0].shape[0]
    half = keep_out.shape[0]
    grads = []
    for i in range(groups):
        here = pl.ds(i * size, size)
        there = pl.ds((i ^ (groups // 2)) * size, size)
        total = first[here, :].astype(jnp.float32) + second[there, :].astype(jnp.float32)
        aggregated = total.astype(jnp.bfloat16)
        preact = jnp.dot(aggregated, weight[...], preferred_element_type=jnp.float32)
        s = 1.0 / (1.0 + jnp.exp(-preact))
        if i == 0:
            act_out[...] = (preact * s).astype(act_out.dtype)
        slope = cots[i][...].astype(jnp.float32) * s * (1.0 + preact * (1.0 - s))
        slope = slope.astype(jnp.bfloat16)
        grads.append(
            lax.dot_general(
                aggregated, slope, (((0,), (0,)), ((), ())), preferred_element_type=jnp.float32
            )
        )
        back = lax.dot_general(
            slope, weight[...], (((1,), (1,)), ((), ())), preferred_element_type=jnp.float32
        )
        sent_out[here, :] = back.astype(sent_out.dtype)
    grad[...] = tree_sum(grads)
    keep = pl.multiple_of(core * half, half)
    away = pl.multiple_of((1 - core) * half, half)
    keep_out[...] = grad[pl.ds(keep, half), :]
    sent_out[groups * size :, :] = grad[pl.ds(away, half), :].astype(sent_out.dtype)


def layer(first, second, weight, cots, groups):
    span, width = first.shape
    size = cots[0].shape[0]
    return pl.pallas_call(
        functools.partial(layer_kernel, groups),
        out_shape=[
            like((size, width), jnp.bfloat16),
            like((width // 2, width), jnp.float32),
            like((span + width // 2, width), jnp.bfloat16),
        ],
        scratch_shapes=[pltpu.VMEM((width, width), jnp.float32)],
        compiler_params=pltpu.CompilerParams(vmem_limit_bytes=limit_for(first, second, *cots)),
        cost_estimate=pl.CostEstimate(
            flops=6 * span * width * width,
            bytes_accessed=8 * span * width,
            transcendentals=span * width,
        ),
        name="layer",
    )(first, second, weight, *cots)


def scatter_kernel(pieces, own_a, sib_a, own_sent, sib_sent, grad, *outs):
    turned = (((0,), (0,)), ((), ()))
    slots, span, _ = own_a.shape
    for s in range(slots):
        total = lax.dot_general(
            own_a[s], own_sent[:span, :], turned, preferred_element_type=jnp.float32
        ) + lax.dot_general(
            sib_a[s], sib_sent[:span, :], turned, preferred_element_type=jnp.float32
        )
        for (slot, low, high, _, _), out in zip(pieces, outs):
            if slot == s and high > low:
                out[: high - low, :] = total[low:high].astype(out.dtype)
    total = grad[...] + sib_sent[span:, :].astype(jnp.float32)
    for (_, low, high, _, follows), out in zip(pieces, outs):
        if follows:
            out[high - low :, :] = total.astype(out.dtype)


def backward_product(own_a, sib_a, own_sent, sib_sent, grad, pieces):
    slots, span, _ = own_a.shape
    half, width = grad.shape
    return pl.pallas_call(
        functools.partial(scatter_kernel, pieces),
        out_shape=[
            like((high - low + half * follows, width), kind)
            for _, low, high, kind, follows in pieces
        ],
        compiler_params=pltpu.CompilerParams(
            vmem_limit_bytes=limit_for(own_a, sib_a) + slots * span * width * 8
        ),
        cost_estimate=pl.CostEstimate(
            flops=4 * slots * span * span * width,
            bytes_accessed=4 * slots * span * span,
            transcendentals=0,
        ),
        name="backward_product",
    )(own_a, sib_a, own_sent, sib_sent, grad)


def on_device(features, weight, cotangent, tile_row, tile_col, tile_count, tile_vals):
    size, width = features.shape
    groups = lax.axis_size("rep")
    panels = lax.axis_size("blk")
    span = groups * size
    core = lax.axis_index("blk") % 2
    plan = (Halves if Halves.fits(groups, panels) else Direct)(groups, panels)
    slots = sum(len(batch) for batch in plan.batches)

    tiles = (tile_row[0, 0].T, tile_col[0, 0].T, tile_count[0, 0], tile_vals[0, 0])
    meta = jnp.concatenate([tiles[0], tiles[1], tile_count[0]])
    sib_tiles = [along(meta, 1), along(tiles[3], 1)]
    own_a, sib_a = place_tiles(plan, slots, [meta, tiles[3]], sib_tiles, span)
    cots, held = plan.gather(features, cotangent, sib_tiles)

    sums = ()
    for batch in plan.batches:
        sums = forward_product(own_a, sib_a, held, batch, sums, batch is plan.batches[-1])
    own_part, sib_part = sums
    total = (own_part + along(sib_part, 1).astype(jnp.float32)).astype(jnp.bfloat16)
    bit = 1
    while 2 * bit < groups:
        moved = across(total, bit).reshape(groups, size, width)
        moved = moved[jnp.arange(groups) ^ bit].reshape(span, width)
        total = (total.astype(jnp.float32) + moved.astype(jnp.float32)).astype(jnp.bfloat16)
        bit *= 2
    other = across(total, bit)

    activations, grad, sent = layer(total, other, weight, cots, groups)
    pieces = plan.pieces(size, span)
    parts = backward_product(own_a, sib_a, sent, along(sent, 1), grad, pieces)
    feature_grad, grad = plan.scatter(parts, size)
    mate = along(grad, 1)
    weight_grad = jnp.where(
        core == 0, jnp.concatenate([grad, mate]), jnp.concatenate([mate, grad])
    ).astype(jnp.float32) * (1.0 / math.sqrt(size * groups * panels))
    return activations, weight_grad, feature_grad.astype(jnp.bfloat16)


def solution(mesh):
    return jax.shard_map(
        on_device,
        mesh=mesh,
        in_specs=(
            P(BOTH, None),
            P(),
            P(BOTH, None),
            P("rep", "blk", None, None),
            P("rep", "blk", None, None),
            P("rep", "blk", None),
            P("rep", "blk", None, None, None, None),
        ),
        out_specs=(P(BOTH, None), P(), P(BOTH, None)),
        check_vma=False,
    )
```

```python
import functools
import math

import jax
import jax.numpy as jnp
from jax import lax
from jax.experimental import pallas as pl
from jax.experimental.pallas import tpu as pltpu
from jax.sharding import PartitionSpec as P

BOTH = ("rep", "blk")


def xor_pairs(count, bit):
    return [(i, i ^ bit) for i in range(count)]


def tree_sum(terms):
    terms = list(terms)
    while len(terms) > 1:
        terms = [terms[i] + terms[i + 1] for i in range(0, len(terms), 2)]
    return terms[0]


def limit_for(*arrays):
    total = sum(math.prod(a.shape) * a.dtype.itemsize for a in arrays)
    return int(2 * total + (8 << 20))


def like(shape, dtype):
    return jax.ShapeDtypeStruct(shape, dtype)


def after(value, *others):
    return lax.optimization_barrier((value,) + others)[0]


def add_rounded(a, b):
    return (a.astype(jnp.float32) + b.astype(jnp.float32)).astype(a.dtype)


def pairs_of(groups, panels, target, members=None, odd_only=False):
    return [
        (m * panels + p, m * panels + target(m, p) % panels)
        for m in (range(groups) if members is None else members)
        for p in range(panels)
        if not (odd_only and p % 2 == 0)
    ]


def back(pairs):
    return [(b, a) for a, b in pairs]


def move(array, pairs):
    return lax.ppermute(array, BOTH, pairs)


def across(array, bit):
    return lax.ppermute(array, "rep", xor_pairs(lax.axis_size("rep"), bit))


def along(array, bit):
    return lax.ppermute(array, "blk", xor_pairs(lax.axis_size("blk"), bit))


class Direct:
    def __init__(self, groups, panels):
        self.groups, steps = groups, panels // groups
        self.steps = steps
        first = pairs_of(groups, panels, lambda m, p: p + steps * m, range(1, groups))
        last = pairs_of(
            groups, panels, lambda m, p: p + steps * (m + 1), range(groups - 1), odd_only=True
        )
        self.moves = [first, last] + [
            pairs_of(groups, panels, functools.partial(lambda k, m, p: p + steps * m + 2 * k, k))
            for k in range(1, steps // 2)
        ]

        self.batches = [list(range(1 + len(self.moves)))]

    def shifts(self, member, panel):
        steps, groups = self.steps, self.groups
        return [
            (0, True),
            (steps * member, member >= 1),
            (steps * (member + 1), member <= groups - 2),
        ] + [(steps * member + 2 * k, True) for k in range(1, steps // 2)]

    def gather(self, slab, cots, early):
        slabs = [slab] + [across(slab, i) for i in range(1, self.groups)]
        cots = [cots] + [across(cots, i) for i in range(1, self.groups)]
        return cots, [slabs] + [[move(part, pairs) for part in slabs] for pairs in self.moves]

    def pieces(self, size, span):
        moved = [(s, 0, span, jnp.bfloat16, False) for s in range(1, 1 + len(self.moves))]
        return [(0, 0, span, jnp.float32, False)] + moved + [(0, 0, 0, jnp.bfloat16, True)]

    def scatter(self, parts, size):
        column, grad = parts[0], parts[-1]
        for pairs, part in zip(self.moves, parts[1:-1]):
            column = column + move(part, back(pairs)).astype(jnp.float32)
        total = column[:size]
        for i in range(1, self.groups):
            piece = column[i * size : (i + 1) * size].astype(jnp.bfloat16)
            total = total + across(piece, i).astype(jnp.float32)
        bit = 2
        while bit < lax.axis_size("blk"):
            grad = add_rounded(grad, along(grad, bit))
            bit *= 2
        return total, grad


def sends_own():
    return (lax.axis_index("blk") // 2) % 2 == lax.axis_index("rep")


def far_kernel(far, far_mate, came, corner, out):
    size = out.shape[0]
    late = jnp.where(sends_own(), corner[...], came[:size, :]).astype(jnp.float32)
    out[...] = (far[...] + far_mate[...].astype(jnp.float32) + late).astype(out.dtype)


def column_kernel(own, came, corner, ahead, cross, keep_out, pass_out):
    size = keep_out.shape[0]
    slant = jnp.where(sends_own(), came[:size, :], corner[...]).astype(jnp.float32)
    total = own[...] + (ahead[...].astype(jnp.float32) + cross[...].astype(jnp.float32))
    keep_out[...] = total[:size] + slant
    pass_out[...] = total[size:].astype(pass_out.dtype)


def local_call(kernel, name, outs, *arrays):
    moved = sum(a.size * a.dtype.itemsize for a in arrays)
    return pl.pallas_call(
        kernel,
        out_shape=outs,
        compiler_params=pltpu.CompilerParams(vmem_limit_bytes=limit_for(*arrays)),
        cost_estimate=pl.CostEstimate(flops=moved, bytes_accessed=moved, transcendentals=0),
        name=name,
    )(*arrays)


def tails_kernel(first, second, out):
    size = first.shape[0] - out.shape[0]
    total = first[size:, :].astype(jnp.float32) + second[size:, :].astype(jnp.float32)
    out[...] = total.astype(out.dtype)


def add_tails(first, second, size):
    rows, width = first.shape
    return local_call(
        tails_kernel, "add_tails", like((rows - size, width), first.dtype), first, second
    )


def sort_far(far, far_mate, came, corner):
    out = like(far.shape, came.dtype)
    return local_call(far_kernel, "sort_far", out, far, far_mate, came, corner)


def add_column(own, came, corner, ahead, cross):
    outs = [like(corner.shape, jnp.float32), like(corner.shape, corner.dtype)]
    return local_call(column_kernel, "add_column", outs, own, came, corner, ahead, cross)


def finish_kernel(first, second, third, out):
    total = first[...] + second[...].astype(jnp.float32) + third[...].astype(jnp.float32)
    out[...] = total.astype(out.dtype)


def finish(first, second, third):
    return pl.pallas_call(
        finish_kernel,
        out_shape=like(first.shape, second.dtype),
        compiler_params=pltpu.CompilerParams(vmem_limit_bytes=limit_for(first, second, third)),
        cost_estimate=pl.CostEstimate(
            flops=2 * first.size, bytes_accessed=8 * first.size, transcendentals=0
        ),
        name="finish",
    )(first, second, third)


def stack_kernel(first, second, out):
    size = first.shape[0]
    out[:size, :] = first[...]
    out[size:, :] = second[...]


def stack(first, second):
    size, width = first.shape
    return pl.pallas_call(
        stack_kernel,
        out_shape=like((2 * size, width), first.dtype),
        compiler_params=pltpu.CompilerParams(vmem_limit_bytes=limit_for(first, second)),
        cost_estimate=pl.CostEstimate(
            flops=0, bytes_accessed=8 * size * width, transcendentals=0
        ),
        name="stack",
    )(first, second)


class Halves:
    def __init__(self, groups, panels):
        self.panels = panels
        self.ahead = pairs_of(groups, panels, lambda m, p: p + 4 * (1 - 2 * m))
        self.cross = pairs_of(groups, panels, lambda m, p: (p ^ 2) + 4 * (1 - 2 * m))
        self.corner = [(a, b ^ panels) for a, b in pairs_of(groups, panels, lambda m, p: p ^ 2)]
        self.half = pairs_of(groups, panels, lambda m, p: p + panels // 2)

        self.batches = [[0, 2, 3], [1, 4]]

    @staticmethod
    def fits(groups, panels):
        return groups == 2 and panels == 8 * groups

    def shifts(self, member, panel):
        turn = 1 - 2 * member
        other = 1 - 2 * ((panel // 2) % 2)
        crossed = 4 * turn - 2 * other
        last = jnp.where(other == turn, 8 - 2 * other, -2 * other)
        return [(0, True), (self.panels // 2, True), (4 * turn, True), (crossed, True), (last, True)]

    def sends_own(self):
        return (lax.axis_index("blk") // 2) % 2 == lax.axis_index("rep")

    def gather(self, slab, cots, early):
        mate = across(slab, 1)
        cots = [cots, across(cots, 1)]
        far = after(move(slab, self.half), cots[1], *early)
        both = stack(slab, mate)
        ahead = move(both, self.ahead)
        cross = move(both, self.cross)
        own = self.sends_own()
        last = along(jnp.where(own, slab, far), 2)
        last_mate = move(jnp.where(own, far, slab), self.corner)
        return cots, [[both], [far, across(far, 1)], [ahead], [cross], [last, last_mate]]

    def pieces(self, size, span):
        half = jnp.bfloat16
        return [
            (0, 0, span, jnp.float32, False),
            (1, 0, size, jnp.float32, False),
            (1, size, span, half, False),
            (2, 0, span, half, False),
            (3, 0, span, half, False),
            (4, 0, size, half, True),
            (4, size, span, half, False),
        ]

    def scatter(self, parts, size):
        own, far, far_pass, ahead, cross, side, corner = parts
        ahead = move(ahead, back(self.ahead))
        cross = move(cross, back(self.cross))
        came = along(side, 2)
        corner = move(corner, back(self.corner))
        far_mate = across(far_pass, 1)
        grad = add_tails(side, came, size)
        far_sum = sort_far(far, far_mate, came, corner)
        column, column_pass = add_column(own, came, corner, ahead, cross)
        grad = add_rounded(grad, along(grad, 4))
        far_back = move(far_sum, back(self.half))
        mate = across(column_pass, 1)
        result = finish(column, mate, far_back)
        return result, add_rounded(grad, after(along(grad, 8), result))


def place_kernel(plan, groups, panels, *refs):
    member, panel = lax.axis_index("rep"), lax.axis_index("blk")
    shifts = plan.shifts(member, panel)
    offsets = (0, 1 - 2 * (panel % 2))
    for offset, (meta, tiles), out in zip(offsets, (refs[:2], refs[2:4]), refs[4:]):
        steps, cap, size, _ = tiles.shape
        for slot, (shift, had) in enumerate(shifts):
            step = lax.rem(shift - steps * member + offset + 4 * panels, panels)
            live = step < steps if had is True else (step < steps) & had
            there = jnp.where(live, step, 0)
            count = jnp.where(live, meta[2 * cap, there], 0)
            out[slot] = jnp.zeros(out.shape[1:], out.dtype)
            for k in range(cap):

                @pl.when(k < count)
                def _():
                    row = lax.rem(meta[k, there], groups) ^ member
                    col = lax.rem(meta[cap + k, there], groups) ^ member
                    row = pl.multiple_of(row * size, size)
                    col = pl.multiple_of(col * size, size)
                    out[slot, pl.ds(row, size), pl.ds(col, size)] = tiles[there, k]


def place_tiles(plan, slots, own, sib, span):
    tiles = own[1]
    out = like((slots, span, span), tiles.dtype)
    scalars = pl.BlockSpec(memory_space=pltpu.SMEM)
    whole = pl.BlockSpec(memory_space=pltpu.VMEM)
    return pl.pallas_call(
        functools.partial(place_kernel, plan, lax.axis_size("rep"), lax.axis_size("blk")),
        in_specs=[scalars, whole] * 2,
        out_specs=[whole] * 2,
        out_shape=[out, out],
        compiler_params=pltpu.CompilerParams(vmem_limit_bytes=limit_for(out, tiles)),
        cost_estimate=pl.CostEstimate(
            flops=0, bytes_accessed=4 * slots * span * span * 2, transcendentals=0
        ),
        name="place_tiles",
    )(*own, *sib)


def gather_kernel(slots, counts, began, own_a, sib_a, *refs):
    slabs, (own_out, sib_out) = refs[:-2], refs[-2:]
    own = sib = None
    if began:
        (own_in, sib_in), slabs = slabs[:2], slabs[2:]
        own, sib = own_in[...], sib_in[...]
    start = 0
    for s, count in zip(slots, counts):
        panel = [slab[...] for slab in slabs[start : start + count]]
        start += count
        panel = panel[0] if count == 1 else jnp.concatenate(panel, axis=0)
        a = jnp.dot(own_a[s], panel, preferred_element_type=jnp.float32)
        b = jnp.dot(sib_a[s], panel, preferred_element_type=jnp.float32)
        own = a if own is None else own + a
        sib = b if sib is None else sib + b
    own_out[...] = own
    sib_out[...] = sib.astype(sib_out.dtype)


def forward_product(own_a, sib_a, held, slots, sums, last):
    _, span, _ = own_a.shape
    slabs = [slab for s in slots for slab in held[s]]
    width = slabs[0].shape[1]
    return pl.pallas_call(
        functools.partial(gather_kernel, slots, [len(held[s]) for s in slots], bool(sums)),
        out_shape=[
            like((span, width), jnp.float32),
            like((span, width), jnp.bfloat16 if last else jnp.float32),
        ],
        compiler_params=pltpu.CompilerParams(
            vmem_limit_bytes=limit_for(own_a, sib_a, *slabs, *sums)
        ),
        cost_estimate=pl.CostEstimate(
            flops=4 * len(slots) * span * span * width,
            bytes_accessed=4 * len(slots) * span * span,
            transcendentals=0,
        ),
        name="forward_product",
    )(own_a, sib_a, *sums, *slabs)


def layer_kernel(groups, first, second, weight, *refs):
    core = lax.axis_index("blk") % 2
    cots, (act_out, keep_out, sent_out, grad) = refs[:groups], refs[groups:]
    size = cots[0].shape[0]
    half = keep_out.shape[0]
    theirs = [i ^ (groups // 2) for i in range(groups)]
    other = jnp.concatenate([second[i * size : (i + 1) * size, :] for i in theirs], axis=0)
    total = first[...].astype(jnp.float32) + other.astype(jnp.float32)
    aggregated = total.astype(jnp.bfloat16)
    preact = jnp.dot(aggregated, weight[...], preferred_element_type=jnp.float32)
    s = 1.0 / (1.0 + jnp.exp(-preact))
    act_out[...] = (preact[:size] * s[:size]).astype(act_out.dtype)
    cot = jnp.concatenate([c[...] for c in cots], axis=0).astype(jnp.float32)
    slope = (cot * s * (1.0 + preact * (1.0 - s))).astype(jnp.bfloat16)
    rows = slope.shape[0]
    sent_out[:rows, :] = lax.dot_general(
        slope, weight[...], (((1,), (1,)), ((), ())), preferred_element_type=jnp.float32
    ).astype(sent_out.dtype)
    grads = [
        lax.dot_general(
            aggregated[i * size : (i + 1) * size],
            slope[i * size : (i + 1) * size],
            (((0,), (0,)), ((), ())),
            preferred_element_type=jnp.float32,
        )
        for i in range(groups)
    ]
    grad[...] = tree_sum(grads)
    keep = pl.multiple_of(core * half, half)
    away = pl.multiple_of((1 - core) * half, half)
    keep_out[...] = grad[pl.ds(keep, half), :]
    sent_out[groups * size :, :] = grad[pl.ds(away, half), :].astype(sent_out.dtype)


def layer(first, second, weight, cots, groups):
    span, width = first.shape
    size = cots[0].shape[0]
    return pl.pallas_call(
        functools.partial(layer_kernel, groups),
        out_shape=[
            like((size, width), jnp.bfloat16),
            like((width // 2, width), jnp.float32),
            like((span + width // 2, width), jnp.bfloat16),
        ],
        scratch_shapes=[pltpu.VMEM((width, width), jnp.float32)],
        compiler_params=pltpu.CompilerParams(vmem_limit_bytes=limit_for(first, second, *cots)),
        cost_estimate=pl.CostEstimate(
            flops=6 * span * width * width,
            bytes_accessed=8 * span * width,
            transcendentals=span * width,
        ),
        name="layer",
    )(first, second, weight, *cots)


def scatter_kernel(pieces, own_a, sib_a, own_sent, sib_sent, grad, *outs):
    turned = (((0,), (0,)), ((), ()))
    slots, span, _ = own_a.shape
    for s in range(slots):
        total = lax.dot_general(
            own_a[s], own_sent[:span, :], turned, preferred_element_type=jnp.float32
        ) + lax.dot_general(
            sib_a[s], sib_sent[:span, :], turned, preferred_element_type=jnp.float32
        )
        for (slot, low, high, _, _), out in zip(pieces, outs):
            if slot == s and high > low:
                out[: high - low, :] = total[low:high].astype(out.dtype)
    total = grad[...] + sib_sent[span:, :].astype(jnp.float32)
    for (_, low, high, _, follows), out in zip(pieces, outs):
        if follows:
            out[high - low :, :] = total.astype(out.dtype)


def backward_product(own_a, sib_a, own_sent, sib_sent, grad, pieces):
    slots, span, _ = own_a.shape
    half, width = grad.shape
    return pl.pallas_call(
        functools.partial(scatter_kernel, pieces),
        out_shape=[
            like((high - low + half * follows, width), kind)
            for _, low, high, kind, follows in pieces
        ],
        compiler_params=pltpu.CompilerParams(
            vmem_limit_bytes=limit_for(own_a, sib_a) + slots * span * width * 8
        ),
        cost_estimate=pl.CostEstimate(
            flops=4 * slots * span * span * width,
            bytes_accessed=4 * slots * span * span,
            transcendentals=0,
        ),
        name="backward_product",
    )(own_a, sib_a, own_sent, sib_sent, grad)


def on_device(features, weight, cotangent, tile_row, tile_col, tile_count, tile_vals):
    size, width = features.shape
    groups = lax.axis_size("rep")
    panels = lax.axis_size("blk")
    span = groups * size
    core = lax.axis_index("blk") % 2
    plan = (Halves if Halves.fits(groups, panels) else Direct)(groups, panels)
    slots = sum(len(batch) for batch in plan.batches)

    tiles = (tile_row[0, 0].T, tile_col[0, 0].T, tile_count[0, 0], tile_vals[0, 0])
    meta = jnp.concatenate([tiles[0], tiles[1], tile_count[0]])
    sib_tiles = [along(meta, 1), along(tiles[3], 1)]
    own_a, sib_a = place_tiles(plan, slots, [meta, tiles[3]], sib_tiles, span)
    cots, held = plan.gather(features, cotangent, sib_tiles)

    sums = ()
    for batch in plan.batches:
        sums = forward_product(own_a, sib_a, held, batch, sums, batch is plan.batches[-1])
    own_part, sib_part = sums
    total = (own_part + along(sib_part, 1).astype(jnp.float32)).astype(jnp.bfloat16)
    bit = 1
    while 2 * bit < groups:
        moved = across(total, bit).reshape(groups, size, width)
        moved = moved[jnp.arange(groups) ^ bit].reshape(span, width)
        total = (total.astype(jnp.float32) + moved.astype(jnp.float32)).astype(jnp.bfloat16)
        bit *= 2
    other = across(total, bit)

    activations, grad, sent = layer(total, other, weight, cots, groups)
    pieces = plan.pieces(size, span)
    parts = backward_product(own_a, sib_a, sent, along(sent, 1), grad, pieces)
    feature_grad, grad = plan.scatter(parts, size)
    mate = along(grad, 1)
    weight_grad = jnp.where(
        core == 0, jnp.concatenate([grad, mate]), jnp.concatenate([mate, grad])
    ).astype(jnp.float32) * (1.0 / math.sqrt(size * groups * panels))
    return activations, weight_grad, feature_grad.astype(jnp.bfloat16)


def solution(mesh):
    return jax.shard_map(
        on_device,
        mesh=mesh,
        in_specs=(
            P(BOTH, None),
            P(),
            P(BOTH, None),
            P("rep", "blk", None, None),
            P("rep", "blk", None, None),
            P("rep", "blk", None),
            P("rep", "blk", None, None, None, None),
        ),
        out_specs=(P(BOTH, None), P(), P(BOTH, None)),
        check_vma=False,
    )
```

```python
import functools
import math

import jax
import jax.numpy as jnp
from jax import lax
from jax.experimental import pallas as pl
from jax.experimental.pallas import tpu as pltpu
from jax.sharding import PartitionSpec as P

BOTH = ("rep", "blk")


def xor_pairs(count, bit):
    return [(i, i ^ bit) for i in range(count)]


def tree_sum(terms):
    terms = list(terms)
    while len(terms) > 1:
        terms = [terms[i] + terms[i + 1] for i in range(0, len(terms), 2)]
    return terms[0]


def limit_for(*arrays):
    total = sum(math.prod(a.shape) * a.dtype.itemsize for a in arrays)
    return int(2 * total + (8 << 20))


def like(shape, dtype):
    return jax.ShapeDtypeStruct(shape, dtype)


def after(value, *others):
    return lax.optimization_barrier((value,) + others)[0]


def add_rounded(a, b):
    return (a.astype(jnp.float32) + b.astype(jnp.float32)).astype(a.dtype)


def pairs_of(groups, panels, target, members=None, odd_only=False):
    return [
        (m * panels + p, m * panels + target(m, p) % panels)
        for m in (range(groups) if members is None else members)
        for p in range(panels)
        if not (odd_only and p % 2 == 0)
    ]


def back(pairs):
    return [(b, a) for a, b in pairs]


def move(array, pairs):
    return lax.ppermute(array, BOTH, pairs)


def across(array, bit):
    return lax.ppermute(array, "rep", xor_pairs(lax.axis_size("rep"), bit))


def along(array, bit):
    return lax.ppermute(array, "blk", xor_pairs(lax.axis_size("blk"), bit))


class Direct:
    def __init__(self, groups, panels):
        self.groups, steps = groups, panels // groups
        self.steps = steps
        first = pairs_of(groups, panels, lambda m, p: p + steps * m, range(1, groups))
        last = pairs_of(
            groups, panels, lambda m, p: p + steps * (m + 1), range(groups - 1), odd_only=True
        )
        self.moves = [first, last] + [
            pairs_of(groups, panels, functools.partial(lambda k, m, p: p + steps * m + 2 * k, k))
            for k in range(1, steps // 2)
        ]

        self.batches = [list(range(1 + len(self.moves)))]

    def shifts(self, member, panel):
        steps, groups = self.steps, self.groups
        return [
            (0, True),
            (steps * member, member >= 1),
            (steps * (member + 1), member <= groups - 2),
        ] + [(steps * member + 2 * k, True) for k in range(1, steps // 2)]

    def gather(self, slab, cots, early):
        slabs = [slab] + [across(slab, i) for i in range(1, self.groups)]
        cots = [cots] + [across(cots, i) for i in range(1, self.groups)]
        return cots, [slabs] + [[move(part, pairs) for part in slabs] for pairs in self.moves]

    def pieces(self, size, span):
        moved = [(s, 0, span, jnp.bfloat16, False) for s in range(1, 1 + len(self.moves))]
        return [(0, 0, span, jnp.float32, False)] + moved + [(0, 0, 0, jnp.bfloat16, True)]

    def scatter(self, parts, size):
        column, grad = parts[0], parts[-1]
        for pairs, part in zip(self.moves, parts[1:-1]):
            column = column + move(part, back(pairs)).astype(jnp.float32)
        total = column[:size]
        for i in range(1, self.groups):
            piece = column[i * size : (i + 1) * size].astype(jnp.bfloat16)
            total = total + across(piece, i).astype(jnp.float32)
        bit = 2
        while bit < lax.axis_size("blk"):
            grad = add_rounded(grad, along(grad, bit))
            bit *= 2
        return total, grad


def sends_own():
    return (lax.axis_index("blk") // 2) % 2 == lax.axis_index("rep")


def far_kernel(far, far_mate, came, corner, out):
    size = out.shape[0]
    late = jnp.where(sends_own(), corner[...], came[:size, :]).astype(jnp.float32)
    out[...] = (far[...] + far_mate[...].astype(jnp.float32) + late).astype(out.dtype)


def column_kernel(own, came, corner, ahead, cross, keep_out, pass_out):
    size = keep_out.shape[0]
    slant = jnp.where(sends_own(), came[:size, :], corner[...]).astype(jnp.float32)
    total = own[...] + (ahead[...].astype(jnp.float32) + cross[...].astype(jnp.float32))
    keep_out[...] = total[:size] + slant
    pass_out[...] = total[size:].astype(pass_out.dtype)


def local_call(kernel, name, outs, *arrays):
    moved = sum(a.size * a.dtype.itemsize for a in arrays)
    return pl.pallas_call(
        kernel,
        out_shape=outs,
        compiler_params=pltpu.CompilerParams(vmem_limit_bytes=limit_for(*arrays)),
        cost_estimate=pl.CostEstimate(flops=moved, bytes_accessed=moved, transcendentals=0),
        name=name,
    )(*arrays)


def tails_kernel(first, second, out):
    size = first.shape[0] - out.shape[0]
    total = first[size:, :].astype(jnp.float32) + second[size:, :].astype(jnp.float32)
    out[...] = total.astype(out.dtype)


def add_tails(first, second, size):
    rows, width = first.shape
    return local_call(
        tails_kernel, "add_tails", like((rows - size, width), first.dtype), first, second
    )


def sort_far(far, far_mate, came, corner):
    out = like(far.shape, came.dtype)
    return local_call(far_kernel, "sort_far", out, far, far_mate, came, corner)


def add_column(own, came, corner, ahead, cross):
    outs = [like(corner.shape, jnp.float32), like(corner.shape, corner.dtype)]
    return local_call(column_kernel, "add_column", outs, own, came, corner, ahead, cross)


def finish_kernel(first, second, third, out):
    total = first[...] + second[...].astype(jnp.float32) + third[...].astype(jnp.float32)
    out[...] = total.astype(out.dtype)


def finish(first, second, third):
    return pl.pallas_call(
        finish_kernel,
        out_shape=like(first.shape, second.dtype),
        compiler_params=pltpu.CompilerParams(vmem_limit_bytes=limit_for(first, second, third)),
        cost_estimate=pl.CostEstimate(
            flops=2 * first.size, bytes_accessed=8 * first.size, transcendentals=0
        ),
        name="finish",
    )(first, second, third)


def stack_kernel(first, second, out):
    size = first.shape[0]
    out[:size, :] = first[...]
    out[size:, :] = second[...]


def stack(first, second):
    size, width = first.shape
    return pl.pallas_call(
        stack_kernel,
        out_shape=like((2 * size, width), first.dtype),
        compiler_params=pltpu.CompilerParams(vmem_limit_bytes=limit_for(first, second)),
        cost_estimate=pl.CostEstimate(
            flops=0, bytes_accessed=8 * size * width, transcendentals=0
        ),
        name="stack",
    )(first, second)


class Halves:
    def __init__(self, groups, panels):
        self.panels = panels
        self.ahead = pairs_of(groups, panels, lambda m, p: p + 4 * (1 - 2 * m))
        self.cross = pairs_of(groups, panels, lambda m, p: (p ^ 2) + 4 * (1 - 2 * m))
        self.corner = [(a, b ^ panels) for a, b in pairs_of(groups, panels, lambda m, p: p ^ 2)]
        self.half = pairs_of(groups, panels, lambda m, p: p + panels // 2)

        self.batches = [[0, 2, 3], [1, 4]]

    @staticmethod
    def fits(groups, panels):
        return groups == 2 and panels == 8 * groups

    def shifts(self, member, panel):
        turn = 1 - 2 * member
        other = 1 - 2 * ((panel // 2) % 2)
        crossed = 4 * turn - 2 * other
        last = jnp.where(other == turn, 8 - 2 * other, -2 * other)
        return [(0, True), (self.panels // 2, True), (4 * turn, True), (crossed, True), (last, True)]

    def sends_own(self):
        return (lax.axis_index("blk") // 2) % 2 == lax.axis_index("rep")

    def gather(self, slab, cots, early):
        mate = across(slab, 1)
        cots = [cots, across(cots, 1)]
        far = after(move(slab, self.half), cots[1], *early)
        both = stack(slab, mate)
        ahead = move(both, self.ahead)
        cross = move(both, self.cross)
        own = self.sends_own()
        last = along(jnp.where(own, slab, far), 2)
        last_mate = move(jnp.where(own, far, slab), self.corner)
        return cots, [[both], [far, across(far, 1)], [ahead], [cross], [last, last_mate]]

    def pieces(self, size, span):
        half = jnp.bfloat16
        return [
            (0, 0, span, jnp.float32, False),
            (1, 0, size, jnp.float32, False),
            (1, size, span, half, False),
            (2, 0, span, half, False),
            (3, 0, span, half, False),
            (4, 0, size, half, True),
            (4, size, span, half, False),
        ]

    def scatter(self, parts, size):
        own, far, far_pass, ahead, cross, side, corner = parts
        ahead = move(ahead, back(self.ahead))
        cross = move(cross, back(self.cross))
        came = along(side, 2)
        corner = move(corner, back(self.corner))
        far_mate = across(far_pass, 1)
        grad = add_tails(side, came, size)
        far_sum = sort_far(far, far_mate, came, corner)
        column, column_pass = add_column(own, came, corner, ahead, cross)
        grad = add_rounded(grad, along(grad, 4))
        far_back = move(far_sum, back(self.half))
        mate = across(column_pass, 1)
        result = finish(column, mate, far_back)
        return result, add_rounded(grad, after(along(grad, 8), result))


def place_kernel(plan, groups, panels, *refs):
    member, panel = lax.axis_index("rep"), lax.axis_index("blk")
    shifts = plan.shifts(member, panel)
    offsets = (0, 1 - 2 * (panel % 2))
    for offset, (meta, tiles), out in zip(offsets, (refs[:2], refs[2:4]), refs[4:]):
        steps, cap, size, _ = tiles.shape
        for slot, (shift, had) in enumerate(shifts):
            step = lax.rem(shift - steps * member + offset + 4 * panels, panels)
            live = step < steps if had is True else (step < steps) & had
            there = jnp.where(live, step, 0)
            count = jnp.where(live, meta[2 * cap, there], 0)
            out[slot] = jnp.zeros(out.shape[1:], out.dtype)
            for k in range(cap):

                @pl.when(k < count)
                def _():
                    row = lax.rem(meta[k, there], groups) ^ member
                    col = lax.rem(meta[cap + k, there], groups) ^ member
                    row = pl.multiple_of(row * size, size)
                    col = pl.multiple_of(col * size, size)
                    out[slot, pl.ds(row, size), pl.ds(col, size)] = tiles[there, k]


def place_tiles(plan, slots, own, sib, span):
    tiles = own[1]
    out = like((slots, span, span), tiles.dtype)
    scalars = pl.BlockSpec(memory_space=pltpu.SMEM)
    whole = pl.BlockSpec(memory_space=pltpu.VMEM)
    return pl.pallas_call(
        functools.partial(place_kernel, plan, lax.axis_size("rep"), lax.axis_size("blk")),
        in_specs=[scalars, whole] * 2,
        out_specs=[whole] * 2,
        out_shape=[out, out],
        compiler_params=pltpu.CompilerParams(vmem_limit_bytes=limit_for(out, tiles)),
        cost_estimate=pl.CostEstimate(
            flops=0, bytes_accessed=4 * slots * span * span * 2, transcendentals=0
        ),
        name="place_tiles",
    )(*own, *sib)


def gather_kernel(slots, counts, began, own_a, sib_a, *refs):
    slabs, (own_out, sib_out) = refs[:-2], refs[-2:]
    own = sib = None
    if began:
        (own_in, sib_in), slabs = slabs[:2], slabs[2:]
        own, sib = own_in[...], sib_in[...]
    start = 0
    for s, count in zip(slots, counts):
        panel = [slab[...] for slab in slabs[start : start + count]]
        start += count
        panel = panel[0] if count == 1 else jnp.concatenate(panel, axis=0)
        a = jnp.dot(own_a[s], panel, preferred_element_type=jnp.float32)
        b = jnp.dot(sib_a[s], panel, preferred_element_type=jnp.float32)
        own = a if own is None else own + a
        sib = b if sib is None else sib + b
    own_out[...] = own
    sib_out[...] = sib.astype(sib_out.dtype)


def forward_product(own_a, sib_a, held, slots, sums, last):
    _, span, _ = own_a.shape
    slabs = [slab for s in slots for slab in held[s]]
    width = slabs[0].shape[1]
    return pl.pallas_call(
        functools.partial(gather_kernel, slots, [len(held[s]) for s in slots], bool(sums)),
        out_shape=[
            like((span, width), jnp.float32),
            like((span, width), jnp.bfloat16 if last else jnp.float32),
        ],
        compiler_params=pltpu.CompilerParams(
            vmem_limit_bytes=limit_for(own_a, sib_a, *slabs, *sums)
        ),
        cost_estimate=pl.CostEstimate(
            flops=4 * len(slots) * span * span * width,
            bytes_accessed=4 * len(slots) * span * span,
            transcendentals=0,
        ),
        name="forward_product",
    )(own_a, sib_a, *sums, *slabs)


def layer_kernel(groups, first, second, weight, *refs):
    core = lax.axis_index("blk") % 2
    cots, (act_out, keep_out, sent_out, grad) = refs[:groups], refs[groups:]
    size = cots[0].shape[0]
    half = keep_out.shape[0]
    theirs = [i ^ (groups // 2) for i in range(groups)]
    other = jnp.concatenate([second[i * size : (i + 1) * size, :] for i in theirs], axis=0)
    total = first[...].astype(jnp.float32) + other.astype(jnp.float32)
    aggregated = total.astype(jnp.bfloat16)
    preact = jnp.dot(aggregated, weight[...], preferred_element_type=jnp.float32)
    s = 1.0 / (1.0 + jnp.exp(-preact))
    act_out[...] = (preact[:size] * s[:size]).astype(act_out.dtype)
    cot = jnp.concatenate([c[...] for c in cots], axis=0).astype(jnp.float32)
    slope = (cot * s * (1.0 + preact * (1.0 - s))).astype(jnp.bfloat16)
    rows = slope.shape[0]
    sent_out[:rows, :] = lax.dot_general(
        slope, weight[...], (((1,), (1,)), ((), ())), preferred_element_type=jnp.float32
    ).astype(sent_out.dtype)
    grads = [
        lax.dot_general(
            aggregated[i * size : (i + 1) * size],
            slope[i * size : (i + 1) * size],
            (((0,), (0,)), ((), ())),
            preferred_element_type=jnp.float32,
        )
        for i in range(groups)
    ]
    grad[...] = tree_sum(grads)
    keep = pl.multiple_of(core * half, half)
    away = pl.multiple_of((1 - core) * half, half)
    keep_out[...] = grad[pl.ds(keep, half), :]
    sent_out[groups * size :, :] = grad[pl.ds(away, half), :].astype(sent_out.dtype)


def layer(first, second, weight, cots, groups):
    span, width = first.shape
    size = cots[0].shape[0]
    return pl.pallas_call(
        functools.partial(layer_kernel, groups),
        out_shape=[
            like((size, width), jnp.bfloat16),
            like((width // 2, width), jnp.float32),
            like((span + width // 2, width), jnp.bfloat16),
        ],
        scratch_shapes=[pltpu.VMEM((width, width), jnp.float32)],
        compiler_params=pltpu.CompilerParams(vmem_limit_bytes=limit_for(first, second, *cots)),
        cost_estimate=pl.CostEstimate(
            flops=6 * span * width * width,
            bytes_accessed=8 * span * width,
            transcendentals=span * width,
        ),
        name="layer",
    )(first, second, weight, *cots)


def scatter_kernel(pieces, own_a, sib_a, own_sent, sib_sent, grad, *outs):
    turned = (((0,), (0,)), ((), ()))
    slots, span, _ = own_a.shape
    for s in range(slots):
        total = lax.dot_general(
            own_a[s], own_sent[:span, :], turned, preferred_element_type=jnp.float32
        ) + lax.dot_general(
            sib_a[s], sib_sent[:span, :], turned, preferred_element_type=jnp.float32
        )
        for (slot, low, high, _, _), out in zip(pieces, outs):
            if slot == s and high > low:
                out[: high - low, :] = total[low:high].astype(out.dtype)
    total = grad[...] + sib_sent[span:, :].astype(jnp.float32)
    for (_, low, high, _, follows), out in zip(pieces, outs):
        if follows:
            out[high - low :, :] = total.astype(out.dtype)


def backward_product(own_a, sib_a, own_sent, sib_sent, grad, pieces):
    slots, span, _ = own_a.shape
    half, width = grad.shape
    return pl.pallas_call(
        functools.partial(scatter_kernel, pieces),
        out_shape=[
            like((high - low + half * follows, width), kind)
            for _, low, high, kind, follows in pieces
        ],
        compiler_params=pltpu.CompilerParams(
            vmem_limit_bytes=limit_for(own_a, sib_a) + slots * span * width * 8
        ),
        cost_estimate=pl.CostEstimate(
            flops=4 * slots * span * span * width,
            bytes_accessed=4 * slots * span * span,
            transcendentals=0,
        ),
        name="backward_product",
    )(own_a, sib_a, own_sent, sib_sent, grad)


def whole_kernel(scale, mine, theirs, out):
    half = mine.shape[0]
    core = lax.axis_index("blk") % 2
    here = pl.multiple_of(core * half, half)
    there = pl.multiple_of((1 - core) * half, half)
    out[pl.ds(here, half), :] = mine[...].astype(jnp.float32) * scale
    out[pl.ds(there, half), :] = theirs[...].astype(jnp.float32) * scale


def whole_grad(mine, theirs, scale):
    half, width = mine.shape
    out = like((2 * half, width), jnp.float32)
    return local_call(functools.partial(whole_kernel, scale), "whole_grad", out, mine, theirs)


def on_device(features, weight, cotangent, tile_row, tile_col, tile_count, tile_vals):
    size, width = features.shape
    groups = lax.axis_size("rep")
    panels = lax.axis_size("blk")
    span = groups * size
    plan = (Halves if Halves.fits(groups, panels) else Direct)(groups, panels)
    slots = sum(len(batch) for batch in plan.batches)

    tiles = (tile_row[0, 0].T, tile_col[0, 0].T, tile_count[0, 0], tile_vals[0, 0])
    meta = jnp.concatenate([tiles[0], tiles[1], tile_count[0]])
    sib_tiles = [along(meta, 1), along(tiles[3], 1)]
    own_a, sib_a = place_tiles(plan, slots, [meta, tiles[3]], sib_tiles, span)
    cots, held = plan.gather(features, cotangent, sib_tiles)

    sums = ()
    for batch in plan.batches:
        sums = forward_product(own_a, sib_a, held, batch, sums, batch is plan.batches[-1])
    own_part, sib_part = sums
    total = (own_part + along(sib_part, 1).astype(jnp.float32)).astype(jnp.bfloat16)
    bit = 1
    while 2 * bit < groups:
        moved = across(total, bit).reshape(groups, size, width)
        moved = moved[jnp.arange(groups) ^ bit].reshape(span, width)
        total = (total.astype(jnp.float32) + moved.astype(jnp.float32)).astype(jnp.bfloat16)
        bit *= 2
    other = across(total, bit)

    activations, grad, sent = layer(total, other, weight, cots, groups)
    pieces = plan.pieces(size, span)
    parts = backward_product(own_a, sib_a, sent, along(sent, 1), grad, pieces)
    feature_grad, grad = plan.scatter(parts, size)
    mate = along(grad, 1)
    scale = 1.0 / math.sqrt(size * groups * panels)
    weight_grad = whole_grad(grad, mate, scale)
    return activations, weight_grad, feature_grad.astype(jnp.bfloat16)


def solution(mesh):
    return jax.shard_map(
        on_device,
        mesh=mesh,
        in_specs=(
            P(BOTH, None),
            P(),
            P(BOTH, None),
            P("rep", "blk", None, None),
            P("rep", "blk", None, None),
            P("rep", "blk", None),
            P("rep", "blk", None, None, None, None),
        ),
        out_specs=(P(BOTH, None), P(), P(BOTH, None)),
        check_vma=False,
    )
```
